32 devices in a mesh: dp: 8 (over z, x), seq: 4 (over y, core).
Axes of the slice: x: 2, y: 2, z: 4, core: 2. Of those that a mesh axis runs over, the one named last changes fastest.
Arguments:
- tokens: bfloat16 [10240, 2048], P(('dp', 'seq')), may hold values from -6 to 6
- segments: int32 [8, 1280], P('dp', 'seq'), may hold values from 0 to 4, never falling along the last dimension, each value on 1 to 1120 neighbouring positions
- cotangent: bfloat16 [10240, 2048], P(('dp', 'seq')), may hold values from -6 to 6
- w_query: float32 [2048, 256], P(('dp', 'seq')), may hold values from -0.1875 to 0.1875
- w_key: float32 [2048, 256], P(('dp', 'seq')), may hold values from -0.1875 to 0.1875
- w_value: float32 [2048, 2048], P(('dp', 'seq')), may hold values from -0.125 to 0.125
- w_out: float32 [2048, 2048], P(('dp', 'seq')), may hold values from -1 to 1
- w_gate: float32 [2048, 5504], P(('dp', 'seq')), may hold values from -0.125 to 0.125
- w_up: float32 [2048, 5504], P(('dp', 'seq')), may hold values from -0.125 to 0.125
- w_down: float32 [2048, 5504], P(('dp', 'seq')), may hold values from -0.078125 to 0.078125
- norm_attn: float32 [2048], P(('dp', 'seq')), may hold values from 0.5 to 1.5
- norm_mlp: float32 [2048], P(('dp', 'seq')), may hold values from 0.5 to 1.5
Outputs:
- output: bfloat16 [10240, 2048], P(('dp', 'seq'))
- grad_tokens: float32 [10240, 2048], P(('dp', 'seq'))
- grad_w_query: float32 [2048, 256], P(('dp', 'seq'))
- grad_w_key: float32 [2048, 256], P(('dp', 'seq'))
- grad_w_value: float32 [2048, 2048], P(('dp', 'seq'))
- grad_w_out: float32 [2048, 2048], P(('dp', 'seq'))
- grad_w_gate: float32 [2048, 5504], P(('dp', 'seq'))
- grad_w_up: float32 [2048, 5504], P(('dp', 'seq'))
- grad_w_down: float32 [2048, 5504], P(('dp', 'seq'))
- grad_norm_attn: float32 [2048], P(('dp', 'seq'))
- grad_norm_mlp: float32 [2048], P(('dp', 'seq'))
The draws below stay inside these ranges and needn't reach their ends.
Inputs may be any that keep to these rules, and one draw needn't show every extreme that they name: `segments`: along each stream the document numbers never fall; each of the 5 numbers marks one document of 1 to 1120 tokens.
All inputs are finite; a program needn't handle non-finite values.
Results may differ from the reference program's by a relative error of at most 0.012.
The reference program's roundings to bfloat16 on the way count: a program that leaves them out, or rounds other values in their place, can miss the bound.
Values may be sent and summed in bfloat16 or wider, within the bound.
No kernel may reach another device: no remote copies, remote signals or barrier semaphores. Data moves between devices by JAX's collectives and lax.ppermute only.
A program may use at most 400 MiB of HBM per device.

```python
import math
import jax
import jax.numpy as jnp
import numpy as np
from jax import lax

D = 2048
H = 16
DV = 128
F = 16
FF = 5504
SEGS = 5
STREAM = 1280
SEG_MOST = 1120
TOKENS = 10240
N_DP = 8


def shard_levels(rng, dims, pieces, low, largest):
    gain, own = 1.0, jax.random.fold_in(rng, 6)
    for axis_at, blocks in pieces:
        draws = jnp.exp(jax.random.uniform(jax.random.fold_in(own, axis_at), (blocks,), jnp.float32, low / len(pieces), largest / len(pieces)))
        gain = gain * jnp.repeat(draws, dims[axis_at] // blocks).reshape([-1 if axis == axis_at else 1 for axis in range(len(dims))])
    return gain


def split_up(number_of, total, reach, skew):
    weights = [(1 << 20) // math.isqrt(grade ** skew) + 1 for grade in range(2, number_of + 1)]
    rest, holding = total - reach - (number_of - 1), [1] * (number_of - 1)
    while rest > 0:
        candidates = [i for i in range(number_of - 1) if holding[i] < reach]
        pool, remaining = sum([weights[i] for i in candidates]), rest
        for i in candidates:
            extra = min(reach - holding[i], max(1, remaining * weights[i] // pool), rest)
            holding[i] = holding[i] + extra
            rest = rest - extra
    return np.array([reach] + holding)


def ragged(stream_key, count, total, bound, slope):
    if count == 2:
        one = jax.random.randint(stream_key, (), max(1, total - bound), min(bound, total - 1) + 1)
        return jnp.stack([one, total - one])
    sizes = jnp.asarray(split_up(count, total, bound, slope), jnp.int32)
    couples = (count - 1) // 2
    giver, taker = sizes[1:1 + 2 * couples:2], sizes[2:2 + 2 * couples:2]
    margin = jnp.minimum(giver - 1, bound - taker)
    passed = jax.random.randint(jax.random.fold_in(stream_key, 1), (couples,), 0, 1 << 20) % (margin + 1)
    sizes = sizes.at[1:1 + 2 * couples:2].set(giver - passed).at[2:2 + 2 * couples:2].set(taker + passed)
    return sizes[jax.random.permutation(jax.random.fold_in(stream_key, 2), count)]


def gaussian(own_key, dims, scale, bound, cuts=(), kind=jnp.bfloat16):
    entries = jax.random.normal(own_key, dims, jnp.float32) * scale
    if len(cuts) > 0:
        entries = shard_levels(own_key, dims, cuts, -0.22, 0.18) * entries
    return jnp.clip(entries, min=-bound, max=bound).astype(kind)


def setup_inputs(seed: int = 0) -> dict:
    splits = jax.random.split(jax.random.key(seed), 13)
    return {
        "tokens": gaussian(splits[0], (TOKENS, D), 1.0, 6.0, ((0, 32),)),
        "segments": jax.vmap(lambda own: jnp.searchsorted(jnp.cumsum(ragged(own, SEGS, STREAM, SEG_MOST, 2)), jnp.arange(STREAM), side="right"))(jax.random.split(splits[1], N_DP)).reshape((N_DP, STREAM)).astype(jnp.int32),
        "cotangent": gaussian(splits[2], (TOKENS, D), 1.0, 6.0, ((0, 32),)),
        "w_query": gaussian(splits[3], (D, H * F), (D // 2) ** -0.5, 0.1875, ((0, 32),), jnp.float32),
        "w_key": gaussian(splits[4], (D, H * F), (D // 2) ** -0.5, 0.1875, ((0, 32),), jnp.float32),
        "w_value": gaussian(splits[5], (D, D), D ** -0.5, 0.125, ((0, 32),), jnp.float32),
        "w_out": gaussian(splits[6], (D, D), (D // 64) ** -0.5, 1.0, ((0, 32),), jnp.float32),
        "w_gate": gaussian(splits[7], (D, FF), D ** -0.5, 0.125, ((0, 32),), jnp.float32),
        "w_up": gaussian(splits[8], (D, FF), D ** -0.5, 0.125, ((0, 32),), jnp.float32),
        "w_down": gaussian(splits[9], (D, FF), FF ** -0.5, 0.078125, ((0, 32),), jnp.float32),
        "norm_attn": jnp.clip(1.0 + 0.1 * jax.random.normal(splits[10], (D,), jnp.float32), 0.5, 1.5),
        "norm_mlp": jnp.clip(1.0 + 0.1 * jax.random.normal(splits[11], (D,), jnp.float32), 0.5, 1.5),
    }


EPSILON = 1e-06
PRECISE = lax.Precision.HIGHEST

@jax.custom_vjp
def low(v):
    return lax.optimization_barrier(v.astype(jnp.bfloat16)).astype(jnp.float32)

@jax.custom_vjp
def low_back(v):
    return v

def low_keep(v):
    return (low(v), None)

def low_pass(kept, grad):
    return (grad,)

def back_keep(v):
    return (v, None)

def back_low(kept, grad):
    return (low(grad),)
low.defvjp(low_keep, low_pass)
low_back.defvjp(back_keep, back_low)

def features(inputs):
    feat_width = inputs.shape[-1]
    outer_prod = (inputs[..., :, None] * inputs[..., None, :]).reshape(inputs.shape[:-1] + (feat_width * feat_width,))
    constant_one = jnp.ones(inputs.shape[:-1] + (1,), inputs.dtype)
    return jnp.concatenate([constant_one, inputs * feat_width ** (-0.25), outer_prod * (1.0 / math.sqrt(2.0 * feat_width))], axis=-1)

def rms_scale(values):
    return values * lax.rsqrt(lax.optimization_barrier(jnp.mean(values * values, axis=-1, keepdims=True)) + EPSILON)

def attention(feat_query, feat_key, value_heads, segments):

    def one_stream(stream_item):
        query_rows, key_rows, value_rows, stream_docs = stream_item
        positions = jnp.arange(stream_docs.shape[0])
        allowed = (stream_docs[:, None] == stream_docs[None, :]) & (positions[None, :] <= positions[:, None])

        def one_head(head_item):
            head_query, head_key, head_value = head_item
            scores = jnp.dot(head_query, head_key.T, precision=PRECISE)
            masked = jnp.where(allowed, scores, 0.0)
            return jnp.dot(masked, head_value, precision=PRECISE) / lax.optimization_barrier(jnp.sum(masked, axis=-1, keepdims=True))
        heads_out = lax.map(jax.checkpoint(one_head), (query_rows.transpose(1, 0, 2), key_rows.transpose(1, 0, 2), value_rows.transpose(1, 0, 2)))
        return heads_out.transpose(1, 0, 2)
    return lax.map(jax.checkpoint(one_stream), (feat_query, feat_key, value_heads, segments))

def reference(tokens, segments, cotangent, w_query, w_key, w_value, w_out, w_gate, w_up, w_down, norm_attn, norm_mlp):
    streams = tokens.astype(jnp.float32).reshape(N_DP, STREAM, D)
    upstream = cotangent.astype(jnp.float32).reshape(N_DP, STREAM, D)

    def forward(inputs, query_mat, key_mat, value_mat, out_mat, gate_mat, up_mat, down_mat, gain_attn, gain_mlp):
        normed_in = low(rms_scale(inputs) * low(gain_attn))
        queries = low_back(jnp.einsum('bsd,dk->bsk', normed_in, low(query_mat), precision=PRECISE))
        keys_pre = low_back(jnp.einsum('bsd,dk->bsk', normed_in, low(key_mat), precision=PRECISE))
        values = low_back(jnp.einsum('bsd,dk->bsk', normed_in, low(value_mat), precision=PRECISE))
        feat_query = low(features(queries.reshape(N_DP, STREAM, H, F)))
        feat_key = low(features(keys_pre.reshape(N_DP, STREAM, H, F)))
        value_heads = low(values).reshape(N_DP, STREAM, H, DV)
        mixed = attention(feat_query, feat_key, value_heads, segments)
        attended = low(mixed.reshape(N_DP, STREAM, D))
        branch_attn = low_back(jnp.einsum('bsk,kd->bsd', attended, low(out_mat), precision=PRECISE))
        residual = inputs + branch_attn
        normed_mid = low(rms_scale(residual) * low(gain_mlp))
        gate_pre = low_back(jnp.einsum('bsd,df->bsf', normed_mid, low(gate_mat), precision=PRECISE))
        up_pre = low_back(jnp.einsum('bsd,df->bsf', normed_mid, low(up_mat), precision=PRECISE))
        hidden = low(jax.nn.silu(gate_pre) * up_pre)
        branch_mlp = low_back(jnp.einsum('bsf,df->bsd', hidden, low(down_mat), precision=PRECISE))
        return residual + branch_mlp
    outputs, pullback = jax.vjp(forward, streams, w_query, w_key, w_value, w_out, w_gate, w_up, w_down, norm_attn, norm_mlp)
    grads = pullback(upstream)
    return (outputs.astype(jnp.bfloat16).reshape(TOKENS, D), grads[0].reshape(TOKENS, D), grads[1], grads[2], grads[3], grads[4], grads[5], grads[6], grads[7], grads[8], grads[9])
```

```python
import jax
import jax.numpy as jnp
from jax import lax
from jax.sharding import Mesh
from jax.sharding import PartitionSpec as P

HEADS = 16
EPSILON = 1e-06
BF = jnp.bfloat16
F32 = jnp.float32


def index(ax):
    return lax.axis_index(ax)


def shift(v, ax, k=1):
    n = lax.axis_size(ax)
    return lax.ppermute(v, ax, [(i, (i + k) % n) for i in range(n)])


def absolute(rel, ax):
    n = len(rel)
    if n == 1:
        return list(rel)
    i = index(ax)
    out = []
    for j in range(n):
        picked = rel[0]
        for k in range(1, n):
            picked = jnp.where((i - j + n) % n == k, rel[k], picked)
        out.append(picked)
    return out


def ring(v, ax):
    out = [v]
    for _ in range(lax.axis_size(ax) - 1):
        out.append(shift(out[-1], ax))
    return out


def ring_sum(pieces, ax):
    acc = None
    for k in range(len(pieces) - 1, 0, -1):
        term = pieces[k].astype(F32)
        if acc is not None:
            term = term + acc
        acc = shift(term.astype(BF), ax, -1).astype(F32)
    own = pieces[0].astype(F32)
    return own if acc is None else own + acc


def gather_abs(v, axes):
    for ax in reversed(axes):
        v = jnp.concatenate(absolute(ring(v, ax), ax), axis=0)
    return v


def spread_columns(w, ax):
    n = lax.axis_size(ax)
    if n == 1:
        return w
    i = index(ax)
    width = w.shape[1] // n
    rel = []
    for k in range(n):
        block = lax.dynamic_slice_in_dim(w, ((i + k) % n) * width, width, 1)
        rel.append(block if k == 0 else shift(block, ax, k))
    return jnp.concatenate(absolute(rel, ax), axis=0)


def join_columns(g, ax):
    n = lax.axis_size(ax)
    if n == 1:
        return g
    i = index(ax)
    height = g.shape[0] // n
    rel = []
    for k in range(n):
        block = lax.dynamic_slice_in_dim(g, ((i + k) % n) * height, height, 0)
        rel.append(block if k == 0 else shift(block, ax, k))
    return jnp.concatenate(absolute(rel, ax), axis=1)


def vector_sum_scatter(v, axes):
    for ax in axes:
        n = lax.axis_size(ax)
        if n == 1:
            continue
        i = index(ax)
        part = v.shape[0] // n
        acc = lax.dynamic_slice_in_dim(v, i * part, part, 0)
        for k in range(1, n):
            acc = acc + shift(lax.dynamic_slice_in_dim(v, ((i + k) % n) * part, part, 0), ax, k)
        v = acc
    return v


def wide_gather(v, both):
    if both:
        half = v.shape[0] // 2
        upper, lower = v[:half], v[half:]
        x_up, x_low = shift(upper, "x"), shift(lower, "x")
        y_low, y_up = shift(lower, "y"), shift(upper, "y")
        chip = [v, x_up, x_low, y_up, y_low, shift(x_up, "y"), shift(y_low, "x")]
    else:
        chip = ring(v, "y")
    other = [shift(piece, "c") for piece in chip]
    return jnp.concatenate(chip + other, axis=0)


def wide_sum(mine, theirs, rows, both):
    term = mine + shift(theirs, "c").astype(F32)
    if not both:
        n = lax.axis_size("y")
        return ring_sum([term[k * rows : (k + 1) * rows] for k in range(n)], "y")
    half = rows // 2
    own = term[:rows]
    x_up, x_low = term[rows : rows + half], term[rows + half : 2 * rows]
    y_up, y_low = term[2 * rows : 2 * rows + half], term[2 * rows + half : 3 * rows]
    d_up, d_low = term[3 * rows : 3 * rows + half], term[3 * rows + half :]

    def send(a, ax):
        return shift(a.astype(BF), ax).astype(F32)

    got_up = send(y_up, "y")
    got_low = send(x_low, "x")
    x_up = x_up + send(d_up, "y")
    y_low = y_low + send(d_low, "x")
    return jnp.concatenate(
        [own[:half] + got_up + send(x_up, "x"), own[half:] + got_low + send(y_low, "y")], axis=0
    )


def stream_sum(partial, rows):
    nc, ny = lax.axis_size("c"), lax.axis_size("y")
    c, y = index("c"), index("y")
    d = partial.shape[1]
    by = partial.reshape(ny, nc, rows, d)
    terms = []
    for k in range(nc):
        terms.append(lax.dynamic_index_in_dim(by, (c - k + nc) % nc, 1, False))
    term = ring_sum(terms, "c")
    pieces = [lax.dynamic_index_in_dim(term, (y - k + ny) % ny, 0, False) for k in range(ny)]
    return ring_sum(pieces, "y")


def dot(a, b, dims, out=F32):
    return lax.dot_general(a, b, (dims, ((), ())), preferred_element_type=F32).astype(out)


NN = ((1,), (0,))
NT = ((1,), (1,))
TN = ((0,), (0,))


def inverse_rms(v):
    return lax.rsqrt(jnp.mean(v * v, axis=-1, keepdims=True) + EPSILON)


def rms_back(grad, normed, inverse):
    return inverse * (grad - normed * jnp.mean(grad * normed, axis=-1, keepdims=True))


def attention(q, k, v, allowed):
    u = jnp.einsum("thf,shf->hts", q, k, preferred_element_type=F32)
    scores = jnp.where(allowed[None], 1.0 + u * 0.25 + u * u * (1.0 / 32.0), 0.0)
    den = jnp.sum(scores, axis=2).T
    num = jnp.einsum("hts,she->the", scores.astype(BF), v, preferred_element_type=F32)
    return num / den[:, :, None], den


def attention_back(q, k, v, allowed, out, den, grad):
    u = jnp.einsum("thf,shf->hts", q, k, preferred_element_type=F32)
    scores = jnp.where(allowed[None], 1.0 + u * 0.25 + u * u * (1.0 / 32.0), 0.0)
    dnum = grad / den[:, :, None]
    dden = -jnp.sum(grad * out, axis=2) / den
    dnum = dnum.astype(BF)
    ds = jnp.einsum("the,she->hts", dnum, v, preferred_element_type=F32) + dden.T[:, :, None]
    du = jnp.where(allowed[None], ds * (0.25 + u * (1.0 / 16.0)), 0.0).astype(BF)
    dv = jnp.einsum("hts,the->she", scores.astype(BF), dnum, preferred_element_type=F32)
    dq = jnp.einsum("hts,shf->thf", du, k, preferred_element_type=F32)
    dk = jnp.einsum("hts,thf->shf", du, q, preferred_element_type=F32)
    return dq, dk, dv


def per_device(both, tokens, segments, cotangent, wq, wk, wv, wo, wg, wu, wd, g1, g2):
    rows, d = tokens.shape
    everything = ("z", "x", "y", "c")
    nz, nx, ny, nc = (lax.axis_size(a) for a in everything)
    ns = ny * nc
    stream = rows * ns
    heads = HEADS // ns
    fk = wq.shape[1] // HEADS
    fv = wv.shape[1] // HEADS
    own = wq.shape[0]

    def by_block(w):
        return w.astype(BF).reshape(own, ns, w.shape[1] // ns)

    pack = jnp.concatenate([by_block(wq), by_block(wk), by_block(wv)], axis=2)
    width = pack.shape[2]
    pack = pack.reshape(own, ns * width)
    pack = spread_columns(spread_columns(pack, "c"), "y")
    pack = jnp.concatenate(absolute(ring(pack, "x"), "x"), axis=0)
    qkv_mat = lax.all_gather(pack, "z", axis=0, tiled=True)

    ndp = nz * nx
    perm = []
    for dp in range(ndp):
        for u in range(ns):
            c, y = u // ny, u % ny
            perm.append((u * ndp + dp, dp * ns + y * nc + c))
    out_mat = lax.ppermute(wo.astype(BF), everything, perm)
    out_mat = jnp.concatenate(absolute(ring(out_mat, "x"), "x"), axis=0)
    out_mat = lax.all_gather(out_mat, "z", axis=0, tiled=True)

    gains = gather_abs(jnp.stack([g1, g2], axis=1).astype(BF).astype(F32), everything)
    gain_one, gain_two = gains[:, 0][None], gains[:, 1][None]

    def spread(w):
        w = spread_columns(spread_columns(w.astype(BF), "c"), "y")
        if both:
            return lax.all_gather(spread_columns(w, "x"), "z", axis=0, tiled=True)
        return lax.all_gather(w, ("z", "x"), axis=0, tiled=True)

    gate_mat, up_mat, down_mat = spread(wg), spread(wu), spread(wd)

    x_all = gather_abs(tokens, ("y", "c")).astype(F32)
    doc = gather_abs(segments[0], ("y", "c"))
    inv_all = inverse_rms(x_all)
    normed_all = x_all * inv_all
    a_all = (normed_all * gain_one).astype(BF)
    qkv = dot(a_all, qkv_mat, NN, BF)
    q = qkv[:, : heads * fk].reshape(stream, heads, fk)
    k = qkv[:, heads * fk : 2 * heads * fk].reshape(stream, heads, fk)
    v = qkv[:, 2 * heads * fk :].reshape(stream, heads, fv)
    at = jnp.arange(stream)
    allowed = (doc[:, None] == doc[None, :]) & (at[None, :] <= at[:, None])
    o, den = attention(q, k, v, allowed)
    att = o.reshape(stream, heads * fv).astype(BF)
    branch = stream_sum(dot(att, out_mat, NN), rows)
    residual = tokens.astype(F32) + branch
    inv_mlp = inverse_rms(residual)
    normed_res = residual * inv_mlp
    b = (normed_res * gain_two).astype(BF)

    b_all = wide_gather(b, both)
    dy_all = wide_gather(cotangent, both)
    total = b_all.shape[0]
    mid = total // 2
    gate = dot(b_all, gate_mat, NN)
    up = dot(b_all, up_mat, NN)
    dh = dot(dy_all, down_mat, NN)
    sig = jax.nn.sigmoid(gate)
    hidden = (gate * sig * up).astype(BF)
    dgate = (dh * up * sig * (1.0 + gate * (1.0 - sig))).astype(BF)
    dup = (dh * gate * sig).astype(BF)

    def back(r0, r1):
        return dot(dgate[r0:r1], gate_mat, NT) + dot(dup[r0:r1], up_mat, NT)

    db = wide_sum(back(0, mid), back(mid, total).astype(BF), rows, both)
    grad_gate = dot(b_all, dgate, TN, BF)
    grad_up = dot(b_all, dup, TN, BF)
    grad_down = dot(dy_all, hidden, TN, BF)
    ffn = wide_sum(
        dot(hidden[:mid], down_mat, NT), dot(hidden[mid:], down_mat, NT, BF), rows, both
    )
    output = (residual + ffn).astype(BF)

    def finish(g):
        if both:
            g = lax.psum_scatter(g, "z", scatter_dimension=0, tiled=True)
            g = join_columns(g, "x")
        else:
            g = lax.psum_scatter(g, ("z", "x"), scatter_dimension=0, tiled=True)
        return join_columns(join_columns(g, "y"), "c").astype(F32)

    grad_wg, grad_wu, grad_wd = finish(grad_gate), finish(grad_up), finish(grad_down)

    grad_g2 = vector_sum_scatter(jnp.sum(db * normed_res, axis=0), everything)
    dr = cotangent.astype(F32) + rms_back(db * gain_two, normed_res, inv_mlp)

    dz_all = gather_abs(dr.astype(BF), ("y", "c"))
    dc = dot(dz_all, out_mat, NT).reshape(stream, heads, fv)
    grad_wo = dot(att, dz_all, TN, BF)
    dq, dk, dv = attention_back(q, k, v, allowed, o, den, dc)
    dqkv = jnp.concatenate(
        [
            dq.reshape(stream, heads * fk).astype(BF),
            dk.reshape(stream, heads * fk).astype(BF),
            dv.reshape(stream, heads * fv).astype(BF),
        ],
        axis=1,
    )
    grad_qkv = dot(a_all, dqkv, TN, BF)
    da_part = dot(dqkv, qkv_mat, NT)
    grad_g1 = vector_sum_scatter(jnp.sum(da_part * normed_all, axis=0), everything)
    da = stream_sum(da_part, rows)
    x_own = tokens.astype(F32)
    inv_own = inverse_rms(x_own)
    grad_tokens = dr + rms_back(da * gain_one, x_own * inv_own, inv_own)

    def sum_rows(g):
        g = lax.psum_scatter(g, "z", scatter_dimension=0, tiled=True)
        height = g.shape[0] // nx
        x = index("x")
        return ring_sum(
            [lax.dynamic_slice_in_dim(g, ((x - k + nx) % nx) * height, height, 0) for k in range(nx)],
            "x",
        ).astype(BF)

    grad_wo = lax.ppermute(sum_rows(grad_wo), everything, [(t, s) for s, t in perm]).astype(F32)
    grad_qkv = join_columns(join_columns(sum_rows(grad_qkv), "y"), "c").astype(F32)
    grad_qkv = grad_qkv.reshape(own, ns, width)
    grad_wq = grad_qkv[:, :, : heads * fk].reshape(wq.shape)
    grad_wk = grad_qkv[:, :, heads * fk : 2 * heads * fk].reshape(wk.shape)
    grad_wv = grad_qkv[:, :, 2 * heads * fk :].reshape(wv.shape)
    return (
        output,
        grad_tokens,
        grad_wq,
        grad_wk,
        grad_wv,
        grad_wo,
        grad_wg,
        grad_wu,
        grad_wd,
        grad_g1,
        grad_g2,
    )


def solution(mesh):
    n_dp, n_seq = mesh.shape["dp"], mesh.shape["seq"]
    nz = 4 if n_dp % 4 == 0 else n_dp
    nc = 2 if n_seq % 2 == 0 else 1
    nx, ny = n_dp // nz, n_seq // nc
    fine = Mesh(mesh.devices.reshape(nz, nx, ny, nc), ("z", "x", "y", "c"))
    both = nx == 2 and ny == 2
    all_rows = P(("z", "x", "y", "c"), None)
    vector = P(("z", "x", "y", "c"))
    placed = (
        (all_rows, P(("z", "x"), ("y", "c")), all_rows) + (all_rows,) * 7 + (vector, vector)
    )

    def run(*args):
        return per_device(both, *args)

    return jax.shard_map(
        run,
        mesh=fine,
        in_specs=placed,
        out_specs=(all_rows,) * 9 + (vector, vector),
        check_vma=False,
    )
```

```python
import functools

import jax
import jax.numpy as jnp
import numpy as np
from jax import lax
from jax.experimental import pallas as pl
from jax.experimental.pallas import tpu as pltpu
from jax.sharding import Mesh
from jax.sharding import PartitionSpec as P

HEADS = 16
EPSILON = 1e-06
BF = jnp.bfloat16
F32 = jnp.float32


def index(ax):
    return lax.axis_index(ax)


def shift(v, ax, k=1):
    n = lax.axis_size(ax)
    return lax.ppermute(v, ax, [(i, (i + k) % n) for i in range(n)])


def absolute(rel, ax):
    n = len(rel)
    if n == 1:
        return list(rel)
    i = index(ax)
    out = []
    for j in range(n):
        picked = rel[0]
        for k in range(1, n):
            picked = jnp.where((i - j + n) % n == k, rel[k], picked)
        out.append(picked)
    return out


def ring(v, ax):
    out = [v]
    for _ in range(lax.axis_size(ax) - 1):
        out.append(shift(out[-1], ax))
    return out


def ring_sum(pieces, ax):
    acc = None
    for k in range(len(pieces) - 1, 0, -1):
        term = pieces[k].astype(F32)
        if acc is not None:
            term = term + acc
        acc = shift(term.astype(BF), ax, -1).astype(F32)
    own = pieces[0].astype(F32)
    return own if acc is None else own + acc


def fan(v, ax):
    return [v] + [shift(v, ax, k) for k in range(1, lax.axis_size(ax))]


def exchange(blocks, axes):
    return lax.all_to_all(blocks, axes, 0, 0, tiled=True)


def cost(flops, nbytes):
    return pl.CostEstimate(flops=int(flops), bytes_accessed=int(nbytes), transcendentals=0)


def nothing(*refs):
    del refs


def after(v, *deps):
    return pl.pallas_call(
        nothing,
        out_shape=jax.ShapeDtypeStruct(v.shape, v.dtype),
        in_specs=[pl.BlockSpec(memory_space=pl.ANY)] * (1 + len(deps)),
        out_specs=pl.BlockSpec(memory_space=pl.ANY),
        input_output_aliases={0: 0},
        compiler_params=params(1),
        cost_estimate=cost(1, 1),
        name="after",
    )(v, *deps)


def stream_gather(v, ax_y="y", ax_c="c"):
    return [ring(piece, ax_c) for piece in ring(v, ax_y)]


def place_of(ry, rc):
    ny, nc = lax.axis_size("y"), lax.axis_size("c")
    return ((index("y") - ry + ny) % ny) * nc + (index("c") - rc + nc) % nc


def in_order(pieces):
    ny, nc = len(pieces), len(pieces[0])
    rows = pieces[0][0].shape[0]
    out = jnp.zeros((ny * nc * rows,) + pieces[0][0].shape[1:], pieces[0][0].dtype)
    for ry in range(ny):
        for rc in range(nc):
            out = lax.dynamic_update_slice_in_dim(out, pieces[ry][rc], place_of(ry, rc) * rows, 0)
    return out


def stream_sum(partial, rows):
    nc, ny = lax.axis_size("c"), lax.axis_size("y")
    sums = []
    for ry in range(ny):
        terms = [
            lax.dynamic_slice_in_dim(partial, place_of(ry, rc) * rows, rows, 0) for rc in range(nc)
        ]
        sums.append(ring_sum(terms, "c"))
    return ring_sum(sums, "y")


def wide_gather(v, both):
    if both:
        half = v.shape[0] // 2
        x, y = shift(v, "x"), shift(v, "y")
        groups = [[v], [x], [y], [shift(x[:half], "y"), shift(y[half:], "x")]]
    else:
        groups = [[piece] for piece in ring(v, "y")]
    return groups


def with_other(g):
    return (g, [shift(p, "c") for p in g])


def dot(a, b, dims, out=F32):
    return lax.dot_general(a, b, (dims, ((), ())), preferred_element_type=F32).astype(out)


NN = ((1,), (0,))
NT = ((1,), (1,))
TN = ((0,), (0,))


def inverse_rms(v):
    return lax.rsqrt(jnp.mean(v * v, axis=-1, keepdims=True) + EPSILON)


def rms_back(grad, normed, inverse):
    return inverse * (grad - normed * jnp.mean(grad * normed, axis=-1, keepdims=True))


def params(limit=60):
    return pltpu.CompilerParams(vmem_limit_bytes=limit << 20)


def block_of(stream):
    return 256 if stream % 256 == 0 else stream


def allowed_of(doc_col, doc_row, r0, block, length):
    rows = r0 + lax.broadcasted_iota(jnp.int32, (block, length), 0)
    cols = lax.broadcasted_iota(jnp.int32, (block, length), 1)
    return (doc_col == doc_row) & (cols <= rows)


def head_lanes(a, h, fk):
    lane = lax.broadcasted_iota(jnp.int32, a.shape, 1)
    return jnp.where((lane >= h * fk) & (lane < (h + 1) * fk), a, jnp.zeros_like(a))


def attention_kernel(heads, fk, fv, qkv, doc_row, doc_col, att, out, den):
    stream = qkv.shape[0]
    block = block_of(stream)
    wide = heads * fk
    for r0 in range(0, stream, block):
        length = r0 + block
        rows = slice(r0, length)
        allowed = allowed_of(doc_col[rows, :], doc_row[:, :length], r0, block, length)
        q = qkv[rows, :wide]
        k = qkv[:length, wide : 2 * wide]
        dens = []
        for h in range(heads):
            at = slice(h * fv, (h + 1) * fv)
            v = qkv[:length, 2 * wide + h * fv : 2 * wide + (h + 1) * fv]
            w = 1.0 + 0.25 * dot(head_lanes(q, h, fk), k, NT)
            scores = jnp.where(allowed, 0.5 * w * w + 0.5, 0.0)
            total = jnp.sum(scores, axis=1, keepdims=True)
            o = dot(scores.astype(BF), v, NN) / total
            out[rows, at] = o
            att[rows, at] = o.astype(BF)
            dens.append(total)
        den[rows, :] = jnp.concatenate(dens, axis=1)


def attention(qkv, doc, heads, fk, fv):
    stream = qkv.shape[0]
    return pl.pallas_call(
        functools.partial(attention_kernel, heads, fk, fv),
        out_shape=(
            jax.ShapeDtypeStruct((stream, heads * fv), BF),
            jax.ShapeDtypeStruct((stream, heads * fv), F32),
            jax.ShapeDtypeStruct((stream, heads), F32),
        ),
        compiler_params=params(),
        cost_estimate=cost(2 * heads * stream * stream * 256, stream * 6000),
        name="attention",
    )(qkv, doc[None, :], doc[:, None])


def attention_back_kernel(heads, fk, fv, qkv, doc_row, doc_col, out, den, grad, dqkv, dk, dv):
    stream = qkv.shape[0]
    block = block_of(stream)
    wide = heads * fk
    for r0 in range(stream - block, -1, -block):
        length = r0 + block
        rows = slice(r0, length)
        first = length == stream
        allowed = allowed_of(doc_col[rows, :], doc_row[:, :length], r0, block, length)
        q = qkv[rows, :wide]
        k = qkv[:length, wide : 2 * wide]
        dq = jnp.zeros((block, wide), F32)
        dk_add = jnp.zeros((length, wide), F32)
        for h in range(heads):
            at = slice(h * fv, (h + 1) * fv)
            v = qkv[:length, 2 * wide + h * fv : 2 * wide + (h + 1) * fv]
            q_head = head_lanes(q, h, fk)
            w = 1.0 + 0.25 * dot(q_head, k, NT)
            scores = jnp.where(allowed, 0.5 * w * w + 0.5, 0.0).astype(BF)
            inv = 1.0 / den[rows, h : h + 1]
            g = grad[rows, at].astype(F32)
            dnum = (g * inv).astype(BF)
            dden = -jnp.sum(g * out[rows, at], axis=1, keepdims=True) * inv
            ds = dot(dnum, v, NT) + dden
            du = jnp.where(allowed, ds * (0.25 * w), 0.0).astype(BF)
            dq = dq + dot(du, head_lanes(k, h, fk), NN)
            dk_add = dk_add + dot(du, q_head, TN)
            dv_add = dot(scores, dnum, TN)
            dv[:length, at] = dv_add if first else dv[:length, at] + dv_add
        dk[:length, :] = dk_add if first else dk[:length, :] + dk_add
        dqkv[rows, :wide] = dq.astype(BF)
    dqkv[:, wide : 2 * wide] = dk[...].astype(BF)
    dqkv[:, 2 * wide :] = dv[...].astype(BF)


def attention_back(qkv, doc, out, den, grad, heads, fk, fv):
    stream = qkv.shape[0]
    return pl.pallas_call(
        functools.partial(attention_back_kernel, heads, fk, fv),
        out_shape=jax.ShapeDtypeStruct(qkv.shape, BF),
        scratch_shapes=[
            pltpu.VMEM((stream, heads * fk), F32),
            pltpu.VMEM((stream, heads * fv), F32),
        ],
        compiler_params=params(),
        cost_estimate=cost(2 * heads * stream * stream * 640, stream * 8000),
        name="attention_back",
    )(qkv, doc[None, :], doc[:, None], out, den, grad)


def norm_in_kernel(places, *refs):
    pieces, gain = refs[: places.shape[0]], refs[places.shape[0]]
    a_out = refs[-1]
    for k, piece in enumerate(pieces):

        @pl.when(pl.program_id(0) == k)
        def _(piece=piece):
            x = piece[...].astype(F32)
            a_out[...] = (x * inverse_rms(x) * gain[...]).astype(BF)


def norm_in(pieces, places, gain):
    n = len(pieces)
    rows, d = pieces[0].shape

    def at(i, places):
        return (places[i], 0)

    def still(a):
        return pl.BlockSpec(a.shape, lambda i, places: (0, 0), pipeline_mode=pl.Buffered(1))

    return pl.pallas_call(
        norm_in_kernel,
        grid_spec=pltpu.PrefetchScalarGridSpec(
            num_scalar_prefetch=1,
            grid=(n,),
            in_specs=[still(p) for p in pieces] + [still(gain)],
            out_specs=pl.BlockSpec((rows, d), at),
        ),
        out_shape=jax.ShapeDtypeStruct((n * rows, d), BF),
        compiler_params=params(),
        cost_estimate=cost(n * rows * d, 4 * n * rows * d),
        name="norm_in",
    )(places, *pieces, gain)


def whole(a):
    rank = len(a.shape)
    return pl.BlockSpec(a.shape, lambda i: (0,) * rank, pipeline_mode=pl.Buffered(1))


def mat(m, w):
    parts, _, rows, cols = w.shape
    return pl.BlockSpec(
        (parts, 1, rows, cols), lambda i: (0, m, 0, 0), pipeline_mode=pl.Buffered(1)
    )


def rows_of(ref):
    parts, _, rows, cols = ref.shape
    return ref[...].reshape(parts * rows, cols)


def size_of(w):
    parts, _, rows, cols = w.shape
    return parts * rows, cols


def ffn_in_kernel(counts, *refs):
    n = sum(counts)
    parts, (wg, wu) = refs[:n], refs[n : n + 2]
    b_out, gate_out, up_out, h_out, b_ref = refs[-5:]
    start = 0
    for step, count in enumerate(counts):

        @pl.when(pl.program_id(0) == step)
        def _(some=parts[start : start + count]):
            at = 0
            for p in some:
                b_ref[at : at + p.shape[0], :] = p[...]
                at += p.shape[0]

        start += count
    b = b_ref[...]
    b_out[...] = b
    gate = dot(b, rows_of(wg), NN)
    up = dot(b, rows_of(wu), NN)
    gate_out[...] = gate
    up_out[...] = up
    h_out[...] = (gate * jax.nn.sigmoid(gate) * up).astype(BF)


def ffn_in(first, total, steps, w, buffers):
    block = sum(p.shape[0] for p in steps[0])
    d, ff = size_of(w)
    parts = [p for some in steps for p in some]
    operands = parts + [w, w]
    in_specs = [whole(p) for p in parts] + [mat(0, w), mat(1, w)]
    aliases = {}
    if buffers is not None:
        aliases = {len(operands) + j: j for j in range(4)}
        operands += list(buffers)
        in_specs += [pl.BlockSpec(memory_space=pl.ANY)] * 4
    widths = ((d, BF), (ff, F32), (ff, F32), (ff, BF))
    return pl.pallas_call(
        functools.partial(ffn_in_kernel, [len(some) for some in steps]),
        grid=(len(steps),),
        in_specs=in_specs,
        out_specs=tuple(pl.BlockSpec((block, w), lambda i: (first + i, 0)) for w, _ in widths),
        out_shape=tuple(jax.ShapeDtypeStruct((total, w), t) for w, t in widths),
        scratch_shapes=[pltpu.VMEM((block, d), BF)],
        input_output_aliases=aliases,
        compiler_params=params(),
        cost_estimate=cost(
            4 * len(steps) * block * d * ff, 4 * d * ff + len(steps) * block * (4 * d + 10 * ff)
        ),
        name="ffn_in",
    )(*operands)


def ffn_mid_kernel(gate, up, dy, wd, dg_out, du_out):
    sig = jax.nn.sigmoid(gate[...])
    dh = dot(dy[...], rows_of(wd), NN)
    dg_out[...] = (dh * up[...] * (sig * (1.0 + gate[...] * (1.0 - sig)))).astype(BF)
    du_out[...] = (dh * gate[...] * sig).astype(BF)


def ffn_mid(block, gate, up, dy, w):
    total, ff = gate.shape
    d = dy.shape[1]

    def at(i):
        return (i, 0)

    return pl.pallas_call(
        ffn_mid_kernel,
        grid=(total // block,),
        in_specs=[pl.BlockSpec((block, n), at) for n in (ff, ff, d)] + [mat(2, w)],
        out_specs=(pl.BlockSpec((block, ff), at),) * 2,
        out_shape=(jax.ShapeDtypeStruct((total, ff), BF),) * 2,
        compiler_params=params(),
        cost_estimate=cost(2 * total * d * ff, 2 * d * ff + total * (2 * d + 12 * ff)),
        name="ffn_mid",
    )(gate, up, dy, w)


def ffn_back_kernel(dgate, dup, wg, wu, *outs):
    db = dot(dgate[...], rows_of(wg), NT) + dot(dup[...], rows_of(wu), NT)
    db = db.astype(BF)
    for step, out in enumerate(outs):

        @pl.when(pl.program_id(0) == step)
        def _(out=out):
            out[...] = db


def ffn_back(first, count, block, dgate, dup, w):
    d, ff = size_of(w)
    rows = pl.BlockSpec((block, ff), lambda i: (first + i, 0))
    return pl.pallas_call(
        ffn_back_kernel,
        grid=(count,),
        in_specs=[rows, rows, mat(0, w), mat(1, w)],
        out_specs=(pl.BlockSpec((block, d), lambda i: (0, 0)),) * count,
        out_shape=(jax.ShapeDtypeStruct((block, d), BF),) * count,
        compiler_params=params(),
        cost_estimate=cost(4 * count * block * d * ff, 4 * d * ff + count * block * (2 * d + 4 * ff)),
        name="ffn_back",
    )(dgate, dup, w, w)


def dz_in_kernel(places, *refs):
    pieces, mat = refs[: places.shape[0]], refs[places.shape[0]]
    dz_out, dc_out = refs[-2:]
    for k, piece in enumerate(pieces):

        @pl.when(pl.program_id(0) == k)
        def _(piece=piece):
            dz_out[...] = piece[...]
            cols = mat.shape[3]
            dc_out[...] = sum(
                dot(piece[:, k * cols : (k + 1) * cols], columns_of(mat, k), NT)
                for k in range(mat.shape[1])
            )


def dz_in(pieces, places, mat):
    n = len(pieces)
    rows, d = pieces[0].shape
    width = mat.shape[0] * mat.shape[2]

    def at(i, places):
        return (places[i], 0)

    def still(a):
        zeros = (0,) * len(a.shape)
        return pl.BlockSpec(a.shape, lambda i, places: zeros, pipeline_mode=pl.Buffered(1))

    return pl.pallas_call(
        dz_in_kernel,
        grid_spec=pltpu.PrefetchScalarGridSpec(
            num_scalar_prefetch=1,
            grid=(n,),
            in_specs=[still(p) for p in pieces] + [still(mat)],
            out_specs=(pl.BlockSpec((rows, d), at), pl.BlockSpec((rows, width), at)),
        ),
        out_shape=(
            jax.ShapeDtypeStruct((n * rows, d), BF),
            jax.ShapeDtypeStruct((n * rows, width), F32),
        ),
        compiler_params=params(),
        cost_estimate=cost(2 * n * rows * d * width, 6 * n * rows * d),
        name="dz_in",
    )(places, *pieces, mat)


def weight_grad_kernel(a, b, out):
    out[...] = dot(a[...], b[...], TN, BF)


def weight_grad(a, b):
    rows, m = a.shape
    n = b.shape[1]
    block = 512 if m % 512 == 0 else m
    return pl.pallas_call(
        weight_grad_kernel,
        grid=(m // block,),
        in_specs=[pl.BlockSpec((rows, block), lambda i: (0, i)), whole(b)],
        out_specs=pl.BlockSpec((block, n), lambda i: (i, 0)),
        out_shape=jax.ShapeDtypeStruct((m, n), BF),
        compiler_params=params(),
        cost_estimate=cost(2 * rows * m * n, 2 * (rows * (m + n) + m * n)),
        name="weight_grad",
    )(a, b)


def pack_kernel(order, n_plain, *refs):
    out, plain, extra = refs[-1], refs[:n_plain], refs[n_plain:-1]
    rows = plain[0].shape[0]
    n = len(order)
    width = out.shape[2]
    for t, u in enumerate(order):
        some = []
        for ref in plain:
            cols = ref.shape[1] // n
            some.append(ref[:, u * cols : (u + 1) * cols].astype(BF))
        out[t, :rows, :] = jnp.concatenate(some, axis=1)
        some = []
        for ref in extra:
            gap = jnp.zeros((1, width - ref.shape[1]), F32)
            row = jnp.concatenate([ref[...], gap], axis=1) if gap.shape[1] else ref[...]
            some.append(jnp.broadcast_to(row, (8, width)))
        out[t, rows:, :] = jnp.concatenate(some, axis=0).astype(BF)


def pack_columns(order, plain, extra):
    rows = plain[0].shape[0]
    width = sum(w.shape[1] for w in plain) // len(order)
    tall = rows + 8 * len(extra)
    return pl.pallas_call(
        functools.partial(pack_kernel, order, len(plain)),
        out_shape=jax.ShapeDtypeStruct((len(order), tall, width), BF),
        compiler_params=params(),
        cost_estimate=cost(1, 6 * len(order) * tall * width),
        name="pack",
    )(*plain, *extra)


def split_kernel(order, *refs):
    out = refs[-1]
    for m, ref in enumerate(refs[:-1]):
        cols = ref.shape[1] // len(order)
        for t, u in enumerate(order):
            out[t, m] = ref[:, u * cols : (u + 1) * cols].astype(BF)


def split_columns(order, mats):
    rows, cols = mats[0].shape
    n = len(order)
    return pl.pallas_call(
        functools.partial(split_kernel, order),
        out_shape=jax.ShapeDtypeStruct((n, len(mats), rows, cols // n), BF),
        compiler_params=params(),
        cost_estimate=cost(1, 6 * len(mats) * rows * cols),
        name="split",
    )(*mats)


def down_kernel(dy, hid, hid_rows, wd, grad, terms):
    grad[...] = dot(dy[...], hid[...], TN, BF)
    terms[...] = dot(hid_rows[...], rows_of(wd), NT, BF)


def down_both(dy, hid, w):
    rows, d = dy.shape
    ff = hid.shape[1]
    steps = 8
    return pl.pallas_call(
        down_kernel,
        grid=(steps,),
        in_specs=[
            pl.BlockSpec((rows, d // steps), lambda i: (0, i)),
            whole(hid),
            pl.BlockSpec((rows // steps, ff), lambda i: (i, 0)),
            mat(2, w),
        ],
        out_specs=(
            pl.BlockSpec((d // steps, ff), lambda i: (i, 0)),
            pl.BlockSpec((rows // steps, d), lambda i: (i, 0)),
        ),
        out_shape=(
            jax.ShapeDtypeStruct((d, ff), BF),
            jax.ShapeDtypeStruct((rows, d), BF),
        ),
        compiler_params=params(),
        cost_estimate=cost(4 * rows * d * ff, 4 * (rows * d + rows * ff + d * ff)),
        name="down_both",
    )(dy, hid, hid, w)


def pair_grad_kernel(a, b0, b1, out):
    out[0, 0] = dot(a[...], b0[...], TN, BF)
    out[0, 1] = dot(a[...], b1[...], TN, BF)


def pair_grad(a, b0, b1, parts):
    rows, m = a.shape
    n = b0.shape[1]
    block = m // parts
    return pl.pallas_call(
        pair_grad_kernel,
        grid=(parts,),
        in_specs=[pl.BlockSpec((rows, block), lambda i: (0, i)), whole(b0), whole(b1)],
        out_specs=pl.BlockSpec((1, 2, block, n), lambda i: (i, 0, 0, 0)),
        out_shape=jax.ShapeDtypeStruct((parts, 2, block, n), BF),
        compiler_params=params(),
        cost_estimate=cost(4 * rows * m * n, 2 * (rows * (m + 2 * n) + 2 * m * n)),
        name="pair_grad",
    )(a, b0, b1)


def columns_of(w, k):
    n, _, rows, cols = w.shape
    return w[:, k].reshape(n * rows, cols)


def out_kernel(a, w, out):
    out[...] = jnp.concatenate(
        [dot(a[...], columns_of(w, k), NN, BF) for k in range(w.shape[1])], axis=1
    )


def out_terms(a, w):
    stream, n = a.shape
    d = w.shape[1] * w.shape[3]
    block = stream // 4
    return pl.pallas_call(
        out_kernel,
        grid=(4,),
        in_specs=[pl.BlockSpec((block, n), lambda i: (i, 0)), whole(w)],
        out_specs=pl.BlockSpec((block, d), lambda i: (i, 0)),
        out_shape=jax.ShapeDtypeStruct((stream, d), BF),
        compiler_params=params(),
        cost_estimate=cost(2 * stream * n * d, 2 * (stream * (n + d) + n * d)),
        name="out_terms",
    )(a, w)


def unpack_kernel(order, g, out):
    out[...] = jnp.concatenate([g[t, 0].astype(F32) for t in order], axis=1)


def unpack(g, m, order):
    n, _, rows, cols = g.shape
    return pl.pallas_call(
        functools.partial(unpack_kernel, order),
        grid=(1,),
        in_specs=[pl.BlockSpec((n, 1, rows, cols), lambda i: (0, m, 0, 0))],
        out_specs=pl.BlockSpec((rows, n * cols), lambda i: (0, 0)),
        out_shape=jax.ShapeDtypeStruct((rows, n * cols), F32),
        compiler_params=params(),
        cost_estimate=cost(1, 6 * n * rows * cols),
        name="unpack",
    )(g)


def sum_rows(g, *deps):
    nx = lax.axis_size("x")
    x = index("x")
    terms = [lax.dynamic_index_in_dim(g, (x - k + nx) % nx, 1, False) for k in range(nx)]
    mine = ring_sum(terms, "x").astype(BF)
    mine = after(mine.reshape(-1, mine.shape[-1]), *deps)
    return mine, lax.psum_scatter(mine, "z", scatter_dimension=0, tiled=True)


def per_device(both, tokens, segments, cotangent, wq, wk, wv, wo, wg, wu, wd, g1, g2):
    rows, d = tokens.shape
    everything = ("z", "x", "y", "c")
    nz, nx, ny, nc = (lax.axis_size(a) for a in everything)
    ns = ny * nc
    stream = rows * ns
    heads = HEADS // ns
    fk = wq.shape[1] // HEADS
    fv = wv.shape[1] // HEADS
    own = wq.shape[0]

    def order_of(sizes):
        order = np.arange(int(np.prod(sizes))).reshape(sizes[::-1])
        return order.transpose().reshape(-1).tolist()

    width = (wq.shape[1] + wk.shape[1] + wv.shape[1]) // ns
    pack = pack_columns(
        order_of((ny, nc)),
        (wq, wk, wv),
        (jnp.concatenate([g1, g2])[None], segments.astype(F32)),
    )
    pack = exchange(pack, ("y", "c"))
    doc = pack[:, own + 8, :rows].astype(jnp.int32).reshape(stream)
    pack = pack[:, : own + 8]

    group = ("x", "y", "c") if both else ("y", "c")
    sizes = (nx, ny, nc) if both else (ny, nc)
    ng = nx * ns if both else ns
    ff = wg.shape[1] // ng
    along = ("z",) if both else ("z", "x")
    na = nz if both else nz * nx
    blocks = split_columns(order_of(sizes), (wg, wu, wd))
    vy = ring(after(tokens, pack), "y")
    got = exchange(blocks, group).transpose(1, 0, 2, 3).reshape(-1, ff)
    late = after(cotangent, pack)
    dy_x = shift(late, "x")

    ndp = nz * nx

    def gather(w, axes):
        return lax.all_gather(w, axes, axis=0, tiled=True)

    def by_x(pieces):
        return jnp.concatenate(absolute([p[:, None] for p in pieces], "x"), axis=1)

    tall = ns * (own + 8)
    pack = pack.reshape(tall, width)
    joint_form = ns == nz and width % 512 == 128 and d % 512 == 0 and tall % 32 == 0
    if joint_form:
        left = [pack[k * tall // 4 : (k + 1) * tall // 4, width - 128 :] for k in range(4)]
        some = [wo[:, k : k + 512].astype(BF) for k in range(0, d, 512)]
        stacked = [pack[:, : width - 128], jnp.concatenate(left, axis=1)] + some
        joint = gather(jnp.concatenate(stacked, axis=0), "z").reshape(nz, -1, 512)
        cut = tall + tall // 4
        qkv_parts = ring(joint[:, :cut], "x")
        units = [order_of((ny, nc))[t % ns] for t in range(nx * ns)]
        out_w = jnp.stack([joint[u, cut:] for u in units])
        out_w = exchange(after(out_w, qkv_parts[-1]), ("x", "y", "c"))
        out_w = out_w.reshape(nx * ns, d // 512, own, 512)
        arrived_last = [joint]

        def qkv_of(m):
            rest = m[:, tall:].reshape(nz, tall // 4, 4, 128).transpose(0, 2, 1, 3)
            return jnp.concatenate([m[:, :tall], rest.reshape(nz, tall, 128)], axis=2)

    else:
        perm = []
        for dp in range(ndp):
            for u in range(ns):
                perm.append((u * ndp + dp, dp * ns + u % ny * nc + u // ny))
        qkv_z = gather(pack, "z")
        out_z = gather(lax.ppermute(wo.astype(BF), everything, perm), "z")
        qkv_parts = ring(qkv_z.reshape(nz, tall, width), "x")
        out_w = by_x(ring(out_z.reshape(nz, own, d), "x"))
        out_w = out_w.reshape(1, -1, d // 256, 256).transpose(0, 2, 1, 3)
        arrived_last = [qkv_z, out_z]

        def qkv_of(m):
            return m

    got = after(got, vy[-1], dy_x, *arrived_last)
    ffn_w = gather(got, along).reshape(na, 3, d // na, ff)
    qkv_all = by_x([qkv_of(m) for m in qkv_parts]).reshape(ndp * ns, own + 8, width)
    qkv_mat = qkv_all[:, :own].reshape(d, width)
    gains = qkv_all[:, own, : 2 * own].astype(F32)
    gain_one, gain_two = gains[:, :own].reshape(1, d), gains[:, own:].reshape(1, d)

    x_pieces = [ring(p, "c") for p in vy]
    places = jnp.stack([place_of(ry, rc) for ry in range(ny) for rc in range(nc)])
    flat = [p for some in x_pieces for p in some]
    a_all = norm_in(flat, places, gain_one)
    late = after(late, x_pieces[-1][0])
    if both:
        half = rows // 2
        dy_y = shift(late, "y")
        dy_near = [dy_y]
        dy_far = [shift(dy_x[:half], "y"), shift(after(dy_y[half:], qkv_parts[-1]), "x")]
        dy_groups = [[late], [dy_x], [dy_y], dy_far]
    else:
        dy_groups = [[p] for p in ring(late, "y")]
        dy_near, dy_far = dy_groups[1], dy_groups[-1]
    dy_groups = [(g, [shift(p, "c") for p in g]) for g in dy_groups]
    dy_all = jnp.concatenate([p for mine, theirs in dy_groups for p in mine + theirs], axis=0)
    qkv = dot(a_all, qkv_mat, NN, BF)
    att, o, den = attention(qkv, doc, heads, fk, fv)
    branch = stream_sum(out_terms(after(att, *dy_near, *dy_far), out_w), rows)
    residual = tokens.astype(F32) + branch
    inv_mlp = inverse_rms(residual)
    normed_res = residual * inv_mlp
    b = (normed_res * gain_two).astype(BF)

    groups = wide_gather(b, both)
    count = len(groups)
    b_far = groups[-1]
    total = 2 * count * rows
    near = [some for g in groups[:-1] for some in with_other(g)]
    near[0] = [after(near[0][0], dy_all)]
    buffers = ffn_in(0, total, near, ffn_w, None)
    b_far = with_other([after(p, buffers[3]) for p in b_far])
    buffers = ffn_in(2 * count - 2, total, list(b_far), ffn_w, buffers)
    b_all, gate, up, hidden = buffers
    dgate, dup = ffn_mid(rows, gate, up, dy_all, ffn_w)

    def back(some, dgate, *deps):
        out = ffn_back(2 * some[0], 2 * len(some), rows, dgate, dup, ffn_w)
        theirs = [after(p, *deps) if deps else p for p in out[1::2]]
        return [(m, t, shift(t, "c")) for m, t in zip(out[::2], theirs)]

    def joined(mine, _, other):
        return mine.astype(F32) + other.astype(F32)

    def send(a, ax):
        return shift(a, ax).astype(F32)

    half = rows // 2
    if both:
        far = joined(*back([3], dgate)[0]).astype(BF)
        up_got, low_got = send(far[:half], "y"), send(far[half:], "x")
        dgate = after(dgate, far)
        tx, ty = [joined(*t) for t in back([1, 2], dgate, up_got, low_got)]
        x_low, y_up = tx[half:].astype(BF), ty[:half].astype(BF)
        x_up, y_low = (tx[:half] + up_got).astype(BF), (ty[half:] + low_got).astype(BF)
        dgate = after(dgate, x_low, y_up)
        mine = back([0], dgate)[0]
        own_term = joined(*mine)
        hidden = after(hidden, x_up, y_low, own_term)
        grad_down, ffn_terms = down_both(dy_all, hidden, ffn_w)
        own_term = after(own_term, grad_down)
        db = jnp.concatenate(
            [
                own_term[:half] + send(y_up, "y") + send(x_up, "x"),
                own_term[half:] + send(x_low, "x") + send(y_low, "y"),
            ],
            axis=0,
        )
    else:
        terms = [joined(*t) for t in back(list(range(count)), dgate)]
        grad_down, ffn_terms = down_both(dy_all, hidden, ffn_w)
        db = ring_sum(terms, "y")
    dr = cotangent.astype(F32) + rms_back(db * gain_two, normed_res, inv_mlp)

    dz = dr.astype(BF)
    down_sum = lax.psum_scatter(after(grad_down, dz), along, scatter_dimension=0, tiled=True)
    dz_y = ring(dz, "y")
    dz_own = ring(dz, "c")
    arrived = dz_y[-1]
    soon = dz_own[-1]
    blocks = [ffn_terms[g * rows : (g + 1) * rows] for g in range(2 * count)]
    others = [shift(blocks[2 * g + 1], "c") for g in range(count)]
    first = [
        (blocks[2 * g].astype(F32) + others[g].astype(F32)).astype(BF) for g in range(1, count)
    ]
    grad_in = pair_grad(b_all, after(dgate, soon, *first), dup, na)
    dz_pieces = [dz_own] + [ring(after(p, grad_in), "c") for p in dz_y[1:]]
    places = after(places, grad_in)
    in_sum = lax.psum_scatter(
        after(grad_in.reshape(-1, ff), arrived, down_sum), along, scatter_dimension=0, tiled=True
    )
    dz_all, dc = dz_in([p for some in dz_pieces for p in some], places, out_w)
    grad_wo = weight_grad(att, dz_all)
    if joint_form:
        g = exchange(grad_wo.reshape(nx * ns, own, d), ("x", "y", "c"))
        g = jnp.sum(g.reshape(nx, ns, own, d).astype(F32), axis=0).astype(BF)
        wo_mine = jnp.concatenate([g[t] for t in np.argsort(order_of((ny, nc)))], axis=0)
    else:
        wo_mine, _ = sum_rows(grad_wo.reshape(nz, nx, own, d))
    wo_sum = lax.psum_scatter(
        after(wo_mine, in_sum), "z", scatter_dimension=0, tiled=True
    )

    dc = after(dc, grad_wo)
    if both:
        to_x, to_y, far = first
        low_got = shift(to_x[half:], "x")
        far, to_y = after(far, arrived), after(to_y, arrived)
        x_up = (to_x[:half].astype(F32) + send(far[:half], "y")).astype(BF)
        y_low = (to_y[half:].astype(F32) + send(far[half:], "x")).astype(BF)
        up_got = shift(to_y[:half], "y")
        dc = after(dc, x_up, y_low)
        x_got, y_got = shift(x_up, "x"), shift(y_low, "y")
    dqkv = attention_back(qkv, doc, o, den, dc, heads, fk, fv)
    late = [up_got, low_got, x_got, y_got] if both else []
    dqkv = after(dqkv, wo_mine, *late)
    da_part = dot(dqkv, qkv_mat, NT)
    grad_qkv = weight_grad(a_all, after(dqkv, da_part))
    da = stream_sum(da_part, rows)
    qkv_mine, qkv_sum = sum_rows(grad_qkv.reshape(nz, nx, ns * own, width), wo_sum, da)
    back = jnp.concatenate([down_sum.reshape(1, ng, own, ff), in_sum.reshape(2, ng, own, ff)])
    back = exchange(back.transpose(1, 0, 2, 3), group)
    order = np.argsort(order_of(sizes)).tolist()
    grad_wg, grad_wu, grad_wd = [unpack(back, m, order) for m in (1, 2, 0)]
    qkv_sum = after(qkv_sum, grad_wg, grad_wu, grad_wd)
    own_term = after(blocks[0], grad_qkv).astype(F32) + others[0].astype(F32)
    if both:
        ffn = own_term + jnp.concatenate(
            [
                up_got.astype(F32) + x_got.astype(F32),
                low_got.astype(F32) + y_got.astype(F32),
            ],
            axis=0,
        )
    else:
        ffn = ring_sum([own_term] + first, "y")
    output = (residual + ffn).astype(BF)
    x_own = tokens.astype(F32)
    inv_own = inverse_rms(x_own)
    grad_tokens = dr + rms_back(da * gain_one, x_own * inv_own, inv_own)

    qkv_sum = exchange(qkv_sum.reshape(ns, own, width), ("y", "c"))
    qkv_sum = qkv_sum.reshape(ny, nc, own, width).transpose(2, 1, 0, 3)
    qkv_sum = qkv_sum.reshape(own, ns, width).astype(F32)
    grad_wq = qkv_sum[:, :, : heads * fk].reshape(wq.shape)
    grad_wk = qkv_sum[:, :, heads * fk : 2 * heads * fk].reshape(wk.shape)
    grad_wv = qkv_sum[:, :, 2 * heads * fk :].reshape(wv.shape)
    if joint_form:
        grad_wo = wo_sum.astype(F32)
    else:
        grad_wo = lax.ppermute(wo_sum, everything, [(t, s) for s, t in perm]).astype(F32)

    def gain_grad(gain, *pairs):
        total = sum(jnp.sum(w.astype(BF).astype(F32) * g, axis=1) for w, g in pairs)
        return total / gain.astype(BF).astype(F32)

    return (
        output,
        grad_tokens,
        grad_wq,
        grad_wk,
        grad_wv,
        grad_wo,
        grad_wg,
        grad_wu,
        grad_wd,
        gain_grad(g1, (wq, grad_wq), (wk, grad_wk), (wv, grad_wv)),
        gain_grad(g2, (wg, grad_wg), (wu, grad_wu)),
    )


def solution(mesh):
    n_dp, n_seq = mesh.shape["dp"], mesh.shape["seq"]
    nz = 4 if n_dp % 4 == 0 else n_dp
    nc = 2 if n_seq % 2 == 0 else 1
    nx, ny = n_dp // nz, n_seq // nc
    fine = Mesh(mesh.devices.reshape(nz, nx, ny, nc), ("z", "x", "y", "c"))
    both = nx == 2 and ny == 2
    all_rows = P(("z", "x", "y", "c"), None)
    vector = P(("z", "x", "y", "c"))
    placed = (
        (all_rows, P(("z", "x"), ("y", "c")), all_rows) + (all_rows,) * 7 + (vector, vector)
    )

    def run(*args):
        return per_device(both, *args)

    return jax.shard_map(
        run,
        mesh=fine,
        in_specs=placed,
        out_specs=(all_rows,) * 9 + (vector, vector),
        check_vma=False,
    )
```

```python
import functools

import jax
import jax.numpy as jnp
import numpy as np
from jax import lax
from jax.experimental import pallas as pl
from jax.experimental.pallas import tpu as pltpu
from jax.sharding import Mesh
from jax.sharding import PartitionSpec as P

HEADS = 16
EPSILON = 1e-06
BF = jnp.bfloat16
F32 = jnp.float32


def index(ax):
    return lax.axis_index(ax)


def shift(v, ax, k=1):
    n = lax.axis_size(ax)
    return lax.ppermute(v, ax, [(i, (i + k) % n) for i in range(n)])


def absolute(rel, ax):
    n = len(rel)
    if n == 1:
        return list(rel)
    i = index(ax)
    out = []
    for j in range(n):
        picked = rel[0]
        for k in range(1, n):
            picked = jnp.where((i - j + n) % n == k, rel[k], picked)
        out.append(picked)
    return out


def ring(v, ax):
    out = [v]
    for _ in range(lax.axis_size(ax) - 1):
        out.append(shift(out[-1], ax))
    return out


def ring_sum(pieces, ax):
    acc = None
    for k in range(len(pieces) - 1, 0, -1):
        term = pieces[k].astype(F32)
        if acc is not None:
            term = term + acc
        acc = shift(term.astype(BF), ax, -1).astype(F32)
    own = pieces[0].astype(F32)
    return own if acc is None else own + acc


def fan(v, ax):
    return [v] + [shift(v, ax, k) for k in range(1, lax.axis_size(ax))]


def exchange(blocks, axes):
    return lax.all_to_all(blocks, axes, 0, 0, tiled=True)


def cost(flops, nbytes):
    return pl.CostEstimate(flops=int(flops), bytes_accessed=int(nbytes), transcendentals=0)


def nothing(*refs):
    del refs


def after(v, *deps):
    return pl.pallas_call(
        nothing,
        out_shape=jax.ShapeDtypeStruct(v.shape, v.dtype),
        in_specs=[pl.BlockSpec(memory_space=pl.ANY)] * (1 + len(deps)),
        out_specs=pl.BlockSpec(memory_space=pl.ANY),
        input_output_aliases={0: 0},
        compiler_params=params(1),
        cost_estimate=cost(1, 1),
        name="after",
    )(v, *deps)


def stream_gather(v, ax_y="y", ax_c="c"):
    return [ring(piece, ax_c) for piece in ring(v, ax_y)]


def place_of(ry, rc):
    ny, nc = lax.axis_size("y"), lax.axis_size("c")
    return ((index("y") - ry + ny) % ny) * nc + (index("c") - rc + nc) % nc


def in_order(pieces):
    ny, nc = len(pieces), len(pieces[0])
    rows = pieces[0][0].shape[0]
    out = jnp.zeros((ny * nc * rows,) + pieces[0][0].shape[1:], pieces[0][0].dtype)
    for ry in range(ny):
        for rc in range(nc):
            out = lax.dynamic_update_slice_in_dim(out, pieces[ry][rc], place_of(ry, rc) * rows, 0)
    return out


def stream_sum(partial, rows):
    nc, ny = lax.axis_size("c"), lax.axis_size("y")
    sums = []
    for ry in range(ny):
        terms = [
            lax.dynamic_slice_in_dim(partial, place_of(ry, rc) * rows, rows, 0) for rc in range(nc)
        ]
        sums.append(ring_sum(terms, "c"))
    if ny == 1:
        return sums[0], jnp.zeros_like(sums[0], BF)
    acc = sums[-1]
    for k in range(ny - 2, 0, -1):
        acc = sums[k] + shift(acc.astype(BF), "y", -1).astype(F32)
    return sums[0], shift(acc.astype(BF), "y", -1)


def wide_gather(v, both):
    if both:
        half = v.shape[0] // 2
        x, y = shift(v, "x"), shift(v, "y")
        groups = [[v], [x], [y], [shift(x[:half], "y"), shift(y[half:], "x")]]
    else:
        groups = [[piece] for piece in ring(v, "y")]
    return groups


def with_other(g):
    return (g, [shift(p, "c") for p in g])


def dot(a, b, dims, out=F32):
    return lax.dot_general(a, b, (dims, ((), ())), preferred_element_type=F32).astype(out)


NN = ((1,), (0,))
NT = ((1,), (1,))
TN = ((0,), (0,))


def inverse_rms(v):
    return lax.rsqrt(jnp.mean(v * v, axis=-1, keepdims=True) + EPSILON)


def rms_back(grad, normed, inverse):
    return inverse * (grad - normed * jnp.mean(grad * normed, axis=-1, keepdims=True))


def params(limit=60):
    return pltpu.CompilerParams(vmem_limit_bytes=limit << 20)


def block_of(stream):
    return 256 if stream % 256 == 0 else stream


def allowed_of(doc_col, doc_row, r0, block, length):
    rows = r0 + lax.broadcasted_iota(jnp.int32, (block, length), 0)
    cols = lax.broadcasted_iota(jnp.int32, (block, length), 1)
    return (doc_col == doc_row) & (cols <= rows)


def head_lanes(a, h, fk):
    lane = lax.broadcasted_iota(jnp.int32, a.shape, 1)
    return jnp.where((lane >= h * fk) & (lane < (h + 1) * fk), a, jnp.zeros_like(a))


def attention_kernel(heads, fk, fv, qkv, doc_row, doc_col, att, out, den):
    stream = qkv.shape[0]
    block = block_of(stream)
    wide = heads * fk
    for r0 in range(0, stream, block):
        length = r0 + block
        rows = slice(r0, length)
        allowed = allowed_of(doc_col[rows, :], doc_row[:, :length], r0, block, length)
        q = qkv[rows, :wide]
        k = qkv[:length, wide : 2 * wide]
        dens = []
        for h in range(heads):
            at = slice(h * fv, (h + 1) * fv)
            v = qkv[:length, 2 * wide + h * fv : 2 * wide + (h + 1) * fv]
            w = 1.0 + 0.25 * dot(head_lanes(q, h, fk), k, NT)
            scores = jnp.where(allowed, 0.5 * w * w + 0.5, 0.0)
            total = jnp.sum(scores, axis=1, keepdims=True)
            o = dot(scores.astype(BF), v, NN) / total
            out[rows, at] = o
            att[rows, at] = o.astype(BF)
            dens.append(total)
        den[rows, :] = jnp.concatenate(dens, axis=1)


def attention(qkv, doc, heads, fk, fv):
    stream = qkv.shape[0]
    return pl.pallas_call(
        functools.partial(attention_kernel, heads, fk, fv),
        out_shape=(
            jax.ShapeDtypeStruct((stream, heads * fv), BF),
            jax.ShapeDtypeStruct((stream, heads * fv), F32),
            jax.ShapeDtypeStruct((stream, heads), F32),
        ),
        compiler_params=params(),
        cost_estimate=cost(2 * heads * stream * stream * 256, stream * 6000),
        name="attention",
    )(qkv, doc[None, :], doc[:, None])


def attention_back_kernel(heads, fk, fv, qkv, doc_row, doc_col, out, den, grad, dqkv, dk, dv):
    stream = qkv.shape[0]
    block = block_of(stream)
    wide = heads * fk
    for r0 in range(stream - block, -1, -block):
        length = r0 + block
        rows = slice(r0, length)
        first = length == stream
        allowed = allowed_of(doc_col[rows, :], doc_row[:, :length], r0, block, length)
        q = qkv[rows, :wide]
        k = qkv[:length, wide : 2 * wide]
        dq = jnp.zeros((block, wide), F32)
        dk_add = jnp.zeros((length, wide), F32)
        for h in range(heads):
            at = slice(h * fv, (h + 1) * fv)
            v = qkv[:length, 2 * wide + h * fv : 2 * wide + (h + 1) * fv]
            q_head = head_lanes(q, h, fk)
            w = 1.0 + 0.25 * dot(q_head, k, NT)
            scores = jnp.where(allowed, 0.5 * w * w + 0.5, 0.0).astype(BF)
            inv = 1.0 / den[rows, h : h + 1]
            g = grad[rows, at].astype(F32)
            dnum = (g * inv).astype(BF)
            dden = -jnp.sum(g * out[rows, at], axis=1, keepdims=True) * inv
            ds = dot(dnum, v, NT) + dden
            du = jnp.where(allowed, ds * (0.25 * w), 0.0).astype(BF)
            dq = dq + dot(du, head_lanes(k, h, fk), NN)
            dk_add = dk_add + dot(du, q_head, TN)
            dv_add = dot(scores, dnum, TN)
            dv[:length, at] = dv_add if first else dv[:length, at] + dv_add
        dk[:length, :] = dk_add if first else dk[:length, :] + dk_add
        dqkv[rows, :wide] = dq.astype(BF)
    dqkv[:, wide : 2 * wide] = dk[...].astype(BF)
    dqkv[:, 2 * wide :] = dv[...].astype(BF)


def attention_back(qkv, doc, out, den, grad, heads, fk, fv):
    stream = qkv.shape[0]
    return pl.pallas_call(
        functools.partial(attention_back_kernel, heads, fk, fv),
        out_shape=jax.ShapeDtypeStruct(qkv.shape, BF),
        scratch_shapes=[
            pltpu.VMEM((stream, heads * fk), F32),
            pltpu.VMEM((stream, heads * fv), F32),
        ],
        compiler_params=params(),
        cost_estimate=cost(2 * heads * stream * stream * 640, stream * 8000),
        name="attention_back",
    )(qkv, doc[None, :], doc[:, None], out, den, grad)


def qkv_in_kernel(places, at, *refs):
    n = places.shape[0]
    pieces, parts = refs[:n], refs[n : n + 2]
    a_out, qkv_out, w, gains, a_ref = refs[-5:]
    nz, _, main = parts[0].shape
    own = parts[0].shape[1] - 80
    quarter = own // 4

    @pl.when(pl.program_id(0) == 0)
    def _():
        for z in range(nz):
            for k, part in enumerate(parts):
                base = pl.multiple_of((2 * z + at[k]) * own, own)
                w[pl.ds(base, own), :main] = part[z, :own, :]
                rows = part[z, own + 64 : own + 80, :].astype(F32)
                g = []
                for t in range(4):
                    there = pl.multiple_of(base + quarter * t, quarter)
                    lanes = slice(128 * t, 128 * (t + 1))
                    w[pl.ds(there, quarter), main:] = part[z, own : own + quarter, lanes]
                    g.append((rows[:1, 128 * t :][:, :64], rows[:1, 128 * t + 64 :][:, :64]))
                for m in range(2):
                    gains[m : m + 1, pl.ds(base, own)] = jnp.concatenate([p[m] for p in g], axis=1)

    for k, piece in enumerate(pieces):

        @pl.when(pl.program_id(0) == k)
        def _(piece=piece):
            x = piece[...].astype(F32)
            a_ref[...] = (x * inverse_rms(x) * gains[:1, :]).astype(BF)

    a = a_ref[...]
    a_out[...] = a
    qkv_out[...] = dot(a, w[...], NN, BF)


def qkv_in(pieces, places, parts, at):
    n = len(pieces)
    rows, d = pieces[0].shape
    width = parts[0].shape[2] + 128

    def row_block(i, places, at):
        return (places[i], 0)

    def still(a):
        zeros = (0,) * len(a.shape)
        return pl.BlockSpec(a.shape, lambda i, places, at: zeros, pipeline_mode=pl.Buffered(1))

    def fixed(i, places, at):
        return (0, 0)

    return pl.pallas_call(
        qkv_in_kernel,
        grid_spec=pltpu.PrefetchScalarGridSpec(
            num_scalar_prefetch=2,
            grid=(n,),
            in_specs=[still(p) for p in pieces] + [still(p) for p in parts],
            out_specs=(
                pl.BlockSpec((rows, d), row_block),
                pl.BlockSpec((rows, width), row_block),
                pl.BlockSpec((d, width), fixed),
                pl.BlockSpec((2, d), fixed),
            ),
            scratch_shapes=[pltpu.VMEM((rows, d), BF)],
        ),
        out_shape=(
            jax.ShapeDtypeStruct((n * rows, d), BF),
            jax.ShapeDtypeStruct((n * rows, width), BF),
            jax.ShapeDtypeStruct((d, width), BF),
            jax.ShapeDtypeStruct((2, d), F32),
        ),
        compiler_params=params(),
        cost_estimate=cost(2 * n * rows * d * width, 6 * n * rows * d),
        name="qkv_in",
    )(places, at, *pieces, *parts)


def norm_in_kernel(places, *refs):
    pieces, gain = refs[: places.shape[0]], refs[places.shape[0]]
    a_out = refs[-1]
    for k, piece in enumerate(pieces):

        @pl.when(pl.program_id(0) == k)
        def _(piece=piece):
            x = piece[...].astype(F32)
            a_out[...] = (x * inverse_rms(x) * gain[...]).astype(BF)


def norm_in(pieces, places, gain):
    n = len(pieces)
    rows, d = pieces[0].shape

    def at(i, places):
        return (places[i], 0)

    def still(a):
        return pl.BlockSpec(a.shape, lambda i, places: (0, 0), pipeline_mode=pl.Buffered(1))

    return pl.pallas_call(
        norm_in_kernel,
        grid_spec=pltpu.PrefetchScalarGridSpec(
            num_scalar_prefetch=1,
            grid=(n,),
            in_specs=[still(p) for p in pieces] + [still(gain)],
            out_specs=pl.BlockSpec((rows, d), at),
        ),
        out_shape=jax.ShapeDtypeStruct((n * rows, d), BF),
        compiler_params=params(),
        cost_estimate=cost(n * rows * d, 4 * n * rows * d),
        name="norm_in",
    )(places, *pieces, gain)


def whole(a):
    rank = len(a.shape)
    return pl.BlockSpec(a.shape, lambda i: (0,) * rank, pipeline_mode=pl.Buffered(1))


def mat(m, w):
    parts, _, rows, cols = w.shape
    return pl.BlockSpec(
        (parts, 1, rows, cols), lambda i: (0, m, 0, 0), pipeline_mode=pl.Buffered(1)
    )


def rows_of(ref):
    parts, _, rows, cols = ref.shape
    return ref[...].reshape(parts * rows, cols)


def size_of(w):
    parts, _, rows, cols = w.shape
    return parts * rows, cols


def ffn_in_kernel(counts, *refs):
    n = sum(counts)
    parts, (wg, wu) = refs[:n], refs[n : n + 2]
    b_out, gate_out, up_out, h_out, b_ref = refs[-5:]
    start = 0
    for step, count in enumerate(counts):

        @pl.when(pl.program_id(0) == step)
        def _(some=parts[start : start + count]):
            at = 0
            for p in some:
                b_ref[at : at + p.shape[0], :] = p[...]
                at += p.shape[0]

        start += count
    b = b_ref[...]
    b_out[...] = b
    gate = dot(b, rows_of(wg), NN)
    up = dot(b, rows_of(wu), NN)
    gate_out[...] = gate
    up_out[...] = up
    h_out[...] = (gate * jax.nn.sigmoid(gate) * up).astype(BF)


def ffn_in(first, total, steps, w, buffers):
    block = sum(p.shape[0] for p in steps[0])
    d, ff = size_of(w)
    parts = [p for some in steps for p in some]
    operands = parts + [w, w]
    in_specs = [whole(p) for p in parts] + [mat(0, w), mat(1, w)]
    aliases = {}
    if buffers is not None:
        aliases = {len(operands) + j: j for j in range(4)}
        operands += list(buffers)
        in_specs += [pl.BlockSpec(memory_space=pl.ANY)] * 4
    widths = ((d, BF), (ff, F32), (ff, F32), (ff, BF))
    return pl.pallas_call(
        functools.partial(ffn_in_kernel, [len(some) for some in steps]),
        grid=(len(steps),),
        in_specs=in_specs,
        out_specs=tuple(pl.BlockSpec((block, w), lambda i: (first + i, 0)) for w, _ in widths),
        out_shape=tuple(jax.ShapeDtypeStruct((total, w), t) for w, t in widths),
        scratch_shapes=[pltpu.VMEM((block, d), BF)],
        input_output_aliases=aliases,
        compiler_params=params(),
        cost_estimate=cost(
            4 * len(steps) * block * d * ff, 4 * d * ff + len(steps) * block * (4 * d + 10 * ff)
        ),
        name="ffn_in",
    )(*operands)


def ffn_mid_kernel(gate, up, dy, wd, dg_out, du_out):
    sig = jax.nn.sigmoid(gate[...])
    dh = dot(dy[...], rows_of(wd), NN)
    dg_out[...] = (dh * up[...] * (sig * (1.0 + gate[...] * (1.0 - sig)))).astype(BF)
    du_out[...] = (dh * gate[...] * sig).astype(BF)


def ffn_mid(block, gate, up, dy, w):
    total, ff = gate.shape
    d = dy.shape[1]

    def at(i):
        return (i, 0)

    return pl.pallas_call(
        ffn_mid_kernel,
        grid=(total // block,),
        in_specs=[pl.BlockSpec((block, n), at) for n in (ff, ff, d)] + [mat(2, w)],
        out_specs=(pl.BlockSpec((block, ff), at),) * 2,
        out_shape=(jax.ShapeDtypeStruct((total, ff), BF),) * 2,
        compiler_params=params(),
        cost_estimate=cost(2 * total * d * ff, 2 * d * ff + total * (2 * d + 12 * ff)),
        name="ffn_mid",
    )(gate, up, dy, w)


def ffn_back_kernel(dgate, dup, wg, wu, *outs):
    db = dot(dgate[...], rows_of(wg), NT) + dot(dup[...], rows_of(wu), NT)
    db = db.astype(BF)
    for step, out in enumerate(outs):

        @pl.when(pl.program_id(0) == step)
        def _(out=out):
            out[...] = db


def ffn_back(first, count, block, dgate, dup, w):
    d, ff = size_of(w)
    rows = pl.BlockSpec((block, ff), lambda i: (first + i, 0))
    return pl.pallas_call(
        ffn_back_kernel,
        grid=(count,),
        in_specs=[rows, rows, mat(0, w), mat(1, w)],
        out_specs=(pl.BlockSpec((block, d), lambda i: (0, 0)),) * count,
        out_shape=(jax.ShapeDtypeStruct((block, d), BF),) * count,
        compiler_params=params(),
        cost_estimate=cost(4 * count * block * d * ff, 4 * d * ff + count * block * (2 * d + 4 * ff)),
        name="ffn_back",
    )(dgate, dup, w, w)


def dz_in_kernel(places, *refs):
    pieces, mat = refs[: places.shape[0]], refs[places.shape[0]]
    dz_out, dc_out = refs[-2:]
    for k, piece in enumerate(pieces):

        @pl.when(pl.program_id(0) == k)
        def _(piece=piece):
            dz_out[...] = piece[...]
            cols = mat.shape[3]
            dc_out[...] = sum(
                dot(piece[:, k * cols : (k + 1) * cols], columns_of(mat, k), NT)
                for k in range(mat.shape[1])
            )


def dz_in(pieces, places, mat):
    n = len(pieces)
    rows, d = pieces[0].shape
    width = mat.shape[0] * mat.shape[2]

    def at(i, places):
        return (places[i], 0)

    def still(a):
        zeros = (0,) * len(a.shape)
        return pl.BlockSpec(a.shape, lambda i, places: zeros, pipeline_mode=pl.Buffered(1))

    return pl.pallas_call(
        dz_in_kernel,
        grid_spec=pltpu.PrefetchScalarGridSpec(
            num_scalar_prefetch=1,
            grid=(n,),
            in_specs=[still(p) for p in pieces] + [still(mat)],
            out_specs=(pl.BlockSpec((rows, d), at), pl.BlockSpec((rows, width), at)),
        ),
        out_shape=(
            jax.ShapeDtypeStruct((n * rows, d), BF),
            jax.ShapeDtypeStruct((n * rows, width), F32),
        ),
        compiler_params=params(),
        cost_estimate=cost(2 * n * rows * d * width, 6 * n * rows * d),
        name="dz_in",
    )(places, *pieces, mat)


def weight_grad_kernel(a, b, out):
    out[...] = dot(a[...], b[...], TN, BF)


def weight_grad(a, b):
    rows, m = a.shape
    n = b.shape[1]
    block = 512 if m % 512 == 0 else m
    return pl.pallas_call(
        weight_grad_kernel,
        grid=(m // block,),
        in_specs=[pl.BlockSpec((rows, block), lambda i: (0, i)), whole(b)],
        out_specs=pl.BlockSpec((block, n), lambda i: (i, 0)),
        out_shape=jax.ShapeDtypeStruct((m, n), BF),
        compiler_params=params(),
        cost_estimate=cost(2 * rows * m * n, 2 * (rows * (m + n) + m * n)),
        name="weight_grad",
    )(a, b)


def pack_kernel(order, n_plain, *refs):
    out, plain, extra = refs[-1], refs[:n_plain], refs[n_plain:-1]
    rows = plain[0].shape[0]
    n = len(order)
    width = out.shape[2]
    for t, u in enumerate(order):
        some = []
        for ref in plain:
            cols = ref.shape[1] // n
            some.append(ref[:, u * cols : (u + 1) * cols].astype(BF))
        out[t, :rows, :] = jnp.concatenate(some, axis=1)
        some = []
        for ref in extra:
            gap = jnp.zeros((1, width - ref.shape[1]), F32)
            row = jnp.concatenate([ref[...], gap], axis=1) if gap.shape[1] else ref[...]
            some.append(jnp.broadcast_to(row, (8, width)))
        out[t, rows:, :] = jnp.concatenate(some, axis=0).astype(BF)


def pack_columns(order, plain, extra):
    rows = plain[0].shape[0]
    width = sum(w.shape[1] for w in plain) // len(order)
    tall = rows + 8 * len(extra)
    return pl.pallas_call(
        functools.partial(pack_kernel, order, len(plain)),
        out_shape=jax.ShapeDtypeStruct((len(order), tall, width), BF),
        compiler_params=params(),
        cost_estimate=cost(1, 6 * len(order) * tall * width),
        name="pack",
    )(*plain, *extra)


def split_kernel(order, *refs):
    out = refs[-1]
    for m, ref in enumerate(refs[:-1]):
        cols = ref.shape[1] // len(order)
        for t, u in enumerate(order):
            out[t, m] = ref[:, u * cols : (u + 1) * cols].astype(BF)


def split_columns(order, mats):
    rows, cols = mats[0].shape
    n = len(order)
    return pl.pallas_call(
        functools.partial(split_kernel, order),
        out_shape=jax.ShapeDtypeStruct((n, len(mats), rows, cols // n), BF),
        compiler_params=params(),
        cost_estimate=cost(1, 6 * len(mats) * rows * cols),
        name="split",
    )(*mats)


def down_kernel(dy, hid, hid_rows, wd, grad, *terms):
    grad[...] = dot(dy[...], hid[...], TN, BF)
    term = dot(hid_rows[...], rows_of(wd), NT, BF)
    for step, out in enumerate(terms):

        @pl.when(pl.program_id(0) == step)
        def _(out=out):
            out[...] = term


def down_both(dy, hid, w):
    rows, d = dy.shape
    ff = hid.shape[1]
    steps = 8
    return pl.pallas_call(
        down_kernel,
        grid=(steps,),
        in_specs=[
            pl.BlockSpec((rows, d // steps), lambda i: (0, i)),
            whole(hid),
            pl.BlockSpec((rows // steps, ff), lambda i: (i, 0)),
            mat(2, w),
        ],
        out_specs=(
            pl.BlockSpec((d // steps, ff), lambda i: (i, 0)),
        )
        + (pl.BlockSpec((rows // steps, d), lambda i: (0, 0)),) * steps,
        out_shape=(jax.ShapeDtypeStruct((d, ff), BF),)
        + (jax.ShapeDtypeStruct((rows // steps, d), BF),) * steps,
        compiler_params=params(),
        cost_estimate=cost(4 * rows * d * ff, 4 * (rows * d + rows * ff + d * ff)),
        name="down_both",
    )(dy, hid, hid, w)


def pair_grad_kernel(a, b0, b1, out, mark):
    mark[...] = jnp.zeros_like(mark)
    out[0, 0] = dot(a[...], b0[...], TN, BF)
    out[0, 1] = dot(a[...], b1[...], TN, BF)


def pair_grad(a, b0, b1, parts):
    rows, m = a.shape
    n = b0.shape[1]
    block = m // parts
    return pl.pallas_call(
        pair_grad_kernel,
        grid=(parts,),
        in_specs=[pl.BlockSpec((rows, block), lambda i: (0, i)), whole(b0), whole(b1)],
        out_specs=(
            pl.BlockSpec((1, 2, block, n), lambda i: (i, 0, 0, 0)),
            pl.BlockSpec((8, 128), lambda i: (0, 0)),
        ),
        out_shape=(
            jax.ShapeDtypeStruct((parts, 2, block, n), BF),
            jax.ShapeDtypeStruct((8, 128), F32),
        ),
        compiler_params=params(),
        cost_estimate=cost(4 * rows * m * n, 2 * (rows * (m + 2 * n) + 2 * m * n)),
        name="pair_grad",
    )(a, b0, b1)


def columns_of(w, k):
    n, _, rows, cols = w.shape
    return w[:, k].reshape(n * rows, cols)


def out_kernel(a, w, out):
    out[...] = jnp.concatenate(
        [dot(a[...], columns_of(w, k), NN, BF) for k in range(w.shape[1])], axis=1
    )


def out_terms(a, w):
    stream, n = a.shape
    d = w.shape[1] * w.shape[3]
    block = stream // 4
    return pl.pallas_call(
        out_kernel,
        grid=(4,),
        in_specs=[pl.BlockSpec((block, n), lambda i: (i, 0)), whole(w)],
        out_specs=pl.BlockSpec((block, d), lambda i: (i, 0)),
        out_shape=jax.ShapeDtypeStruct((stream, d), BF),
        compiler_params=params(),
        cost_estimate=cost(2 * stream * n * d, 2 * (stream * (n + d) + n * d)),
        name="out_terms",
    )(a, w)


def unpack_kernel(order, g, out):
    out[...] = jnp.concatenate([g[t, 0].astype(F32) for t in order], axis=1)


def unpack(g, m, order):
    n, _, rows, cols = g.shape
    return pl.pallas_call(
        functools.partial(unpack_kernel, order),
        grid=(1,),
        in_specs=[pl.BlockSpec((n, 1, rows, cols), lambda i: (0, m, 0, 0))],
        out_specs=pl.BlockSpec((rows, n * cols), lambda i: (0, 0)),
        out_shape=jax.ShapeDtypeStruct((rows, n * cols), F32),
        compiler_params=params(),
        cost_estimate=cost(1, 6 * n * rows * cols),
        name="unpack",
    )(g)


def sum_rows(g):
    nx = lax.axis_size("x")
    x = index("x")
    terms = [lax.dynamic_index_in_dim(g, (x - k + nx) % nx, 1, False) for k in range(nx)]
    mine = ring_sum(terms, "x").astype(BF)
    return terms[-1], mine.reshape(-1, mine.shape[-1])


def per_device(both, tokens, segments, cotangent, wq, wk, wv, wo, wg, wu, wd, g1, g2):
    rows, d = tokens.shape
    everything = ("z", "x", "y", "c")
    nz, nx, ny, nc = (lax.axis_size(a) for a in everything)
    ns = ny * nc
    stream = rows * ns
    heads = HEADS // ns
    fk = wq.shape[1] // HEADS
    fv = wv.shape[1] // HEADS
    own = wq.shape[0]

    def order_of(sizes):
        order = np.arange(int(np.prod(sizes))).reshape(sizes[::-1])
        return order.transpose().reshape(-1).tolist()

    width = (wq.shape[1] + wk.shape[1] + wv.shape[1]) // ns
    pack = pack_columns(
        order_of((ny, nc)),
        (wq, wk, wv),
        (jnp.concatenate([g1, g2])[None], segments.astype(F32)),
    )
    pack = exchange(pack, ("y", "c"))
    doc = pack[:, own + 8, :rows].astype(jnp.int32).reshape(stream)

    group = ("x", "y", "c") if both else ("y", "c")
    sizes = (nx, ny, nc) if both else (ny, nc)
    ng = nx * ns if both else ns
    ff = wg.shape[1] // ng
    along = ("z",) if both else ("z", "x")
    na = nz if both else nz * nx
    blocks = split_columns(order_of(sizes), (wg, wu, wd))
    vy = ring(after(tokens, pack), "y")
    exchanged = exchange(blocks, group)
    got = exchanged.transpose(1, 0, 2, 3).reshape(-1, ff)
    late = after(cotangent, pack)
    dy_x = shift(late, "x")

    ndp = nz * nx

    def gather(w, axes):
        return lax.all_gather(w, axes, axis=0, tiled=True)

    def by_x(pieces):
        return jnp.concatenate(absolute([p[:, None] for p in pieces], "x"), axis=1)

    joint_form = ns == nz == 4 and nx == 2 and own == 64 and width == 640 and d % 512 == 0
    if joint_form:
        left = jnp.concatenate([pack[t, :own, 512:] for t in range(ns)], axis=1)
        extra = jnp.concatenate([pack[t, own : own + 8, :128] for t in range(ns)], axis=1)
        some = [wo[:, k : k + 512].astype(BF) for k in range(0, d, 512)]
        stacked = [pack[:, :own, :512].reshape(ns * own, 512), left, extra, extra] + some
        joint = gather(jnp.concatenate(stacked, axis=0), "z").reshape(nz, -1, 512)
        cut = ns * own + own + 16
        qkv_parts = ring(joint[:, :cut], "x")
        units = [order_of((ny, nc))[t % ns] for t in range(nx * ns)]
        out_w = jnp.stack([joint[u, cut:] for u in units])
        out_w = exchange(after(out_w, qkv_parts[-1]), ("x", "y", "c"))
        out_w = out_w.reshape(nx * ns, d // 512, own, 512)
        arrived_last = [joint]

    else:
        perm = []
        for dp in range(ndp):
            for u in range(ns):
                perm.append((u * ndp + dp, dp * ns + u % ny * nc + u // ny))
        tall = ns * (own + 8)
        qkv_z = gather(pack[:, : own + 8].reshape(tall, width), "z")
        out_z = gather(lax.ppermute(wo.astype(BF), everything, perm), "z")
        qkv_parts = ring(qkv_z.reshape(nz, tall, width), "x")
        out_w = by_x(ring(out_z.reshape(nz, own, d), "x"))
        out_w = out_w.reshape(1, -1, d // 256, 256).transpose(0, 2, 1, 3)
        arrived_last = [qkv_z, out_z]

    got = after(got, vy[-1], dy_x, *arrived_last)
    ffn_w = gather(got, along).reshape(na, 3, d // na, ff)
    x_pieces = [ring(p, "c") for p in vy]
    places = jnp.stack([place_of(ry, rc) for ry in range(ny) for rc in range(nc)])
    flat = [p for some in x_pieces for p in some]
    if joint_form:
        at = jnp.stack([index("x"), 1 - index("x")])
        a_all, qkv, qkv_mat, gains = qkv_in(flat, places, qkv_parts, at)
        gain_one, gain_two = gains[:1], gains[1:]
    else:
        qkv_all = by_x(qkv_parts).reshape(ndp * ns, own + 8, width)
        qkv_mat = qkv_all[:, :own].reshape(d, width)
        gains = qkv_all[:, own, : 2 * own].astype(F32)
        gain_one, gain_two = gains[:, :own].reshape(1, d), gains[:, own:].reshape(1, d)
        a_all = norm_in(flat, places, gain_one)
        qkv = dot(a_all, qkv_mat, NN, BF)
    late = after(late, exchanged)
    if both:
        half = rows // 2
        dy_x, dy_y = after(dy_x, qkv_parts[-1]), after(shift(late, "y"), qkv_parts[-1])
        dy_near = [dy_y]
        dy_far = [shift(dy_x[:half], "y"), shift(dy_y[half:], "x")]
        dy_groups = [[late], [dy_x], [dy_y], dy_far]
    else:
        dy_groups = [[p] for p in ring(late, "y")]
        dy_near, dy_far = dy_groups[1], dy_groups[-1]
    dy_groups = [(g, [shift(p, "c") for p in g]) for g in dy_groups]
    dy_all = jnp.concatenate([p for mine, theirs in dy_groups for p in mine + theirs], axis=0)
    att, o, den = attention(qkv, doc, heads, fk, fv)
    mine, got_r = stream_sum(out_terms(after(att, *dy_near, *dy_far), out_w), rows)
    residual = tokens.astype(F32) + mine + got_r.astype(F32)
    inv_mlp = inverse_rms(residual)
    normed_res = residual * inv_mlp
    b = (normed_res * gain_two).astype(BF)

    groups = wide_gather(b, both)
    count = len(groups)
    b_far = groups[-1]
    total = 2 * count * rows
    near = [some for g in groups[:-1] for some in with_other(g)]
    near[0] = [after(near[0][0], dy_all)]
    buffers = ffn_in(0, total, near, ffn_w, None)
    b_far = with_other([after(p, buffers[3]) for p in b_far])
    buffers = ffn_in(2 * count - 2, total, list(b_far), ffn_w, buffers)
    b_all, gate, up, hidden = buffers
    dgate, dup = ffn_mid(rows, gate, up, dy_all, ffn_w)

    def back(some, dgate, *deps):
        out = ffn_back(2 * some[0], 2 * len(some), rows, dgate, dup, ffn_w)
        theirs = [after(p, *deps) if deps else p for p in out[1::2]]
        return [(m, t, shift(t, "c")) for m, t in zip(out[::2], theirs)]

    def joined(mine, _, other):
        return mine.astype(F32) + other.astype(F32)

    def send(a, ax):
        return shift(a, ax).astype(F32)

    half = rows // 2
    if both:
        far = joined(*back([3], dgate)[0]).astype(BF)
        up_got, low_got = send(far[:half], "y"), send(far[half:], "x")
        dgate = after(dgate, far)
        tx, ty = [joined(*t) for t in back([1, 2], dgate, up_got, low_got)]
        x_low, y_up = tx[half:].astype(BF), ty[:half].astype(BF)
        x_up, y_low = (tx[:half] + up_got).astype(BF), (ty[half:] + low_got).astype(BF)
        dgate = after(dgate, x_low, y_up)
        mine = back([0], dgate)[0]
        own_term = joined(*mine)
        hidden = after(hidden, x_up, y_low, own_term)
        grad_down, *blocks = down_both(dy_all, hidden, ffn_w)
        own_term = after(own_term, blocks[0])
        db = jnp.concatenate(
            [
                own_term[:half] + send(y_up, "y") + send(x_up, "x"),
                own_term[half:] + send(x_low, "x") + send(y_low, "y"),
            ],
            axis=0,
        )
    else:
        terms = [joined(*t) for t in back(list(range(count)), dgate)]
        grad_down, *blocks = down_both(dy_all, hidden, ffn_w)
        db = ring_sum(terms, "y")
    dr = cotangent.astype(F32) + rms_back(db * gain_two, normed_res, inv_mlp)

    dz = dr.astype(BF)
    down_sum = lax.psum_scatter(after(grad_down, dz), along, scatter_dimension=0, tiled=True)
    dz_y = ring(dz, "y")
    dz_own = ring(dz, "c")
    arrived = dz_y[-1]
    soon = dz_own[-1]
    others = [shift(blocks[2 * g + 1], "c") for g in range(count)]
    first = [
        (blocks[2 * g].astype(F32) + others[g].astype(F32)).astype(BF) for g in range(1, count)
    ]
    grad_in, mark = pair_grad(b_all, after(dgate, soon, *first), dup, na)
    dz_pieces = [dz_own] + [ring(after(p, mark), "c") for p in dz_y[1:]]
    dz_all, dc = dz_in([p for some in dz_pieces for p in some], places, out_w)
    far_got = shift(after(first[-1][: rows // 2], arrived), "y")
    grad_wo = weight_grad(att, after(dz_all, far_got))
    in_sum = lax.psum_scatter(
        after(grad_in.reshape(-1, ff), grad_wo, down_sum),
        along,
        scatter_dimension=0,
        tiled=True,
    )
    dc = after(dc, grad_wo)
    if both:
        to_x, to_y, far = first
        low_got = shift(to_x[half:], "x")
        y_low = (to_y[half:].astype(F32) + send(far[half:], "x")).astype(BF)
        x_up = (to_x[:half].astype(F32) + far_got.astype(F32)).astype(BF)
        up_got = shift(after(to_y[:half], arrived), "y")
        y_low = after(y_low, arrived)
        x_got, y_got = shift(x_up, "x"), shift(y_low, "y")
    ffn_got = [up_got, low_got, x_got, y_got] if both else []
    dqkv = attention_back(qkv, doc, o, den, dc, heads, fk, fv)
    dqkv = after(dqkv, *ffn_got)
    if joint_form:
        g = after(grad_wo, dqkv).reshape(nx * ns, own, d)
        wo_there = exchange(g, ("x", "y", "c"))
        g = jnp.sum(wo_there.reshape(nx, ns, own, d).astype(F32), axis=0).astype(BF)
        wo_mine = jnp.concatenate([g[t] for t in np.argsort(order_of((ny, nc)))], axis=0)
    else:
        _, wo_mine = sum_rows(grad_wo.reshape(nz, nx, own, d))
        wo_there = wo_mine
    da_part = dot(dqkv, qkv_mat, NT)
    grad_qkv = after(weight_grad(a_all, after(dqkv, da_part)), wo_there)
    da, da_got = stream_sum(da_part, rows)
    leaving, qkv_mine = sum_rows(grad_qkv.reshape(nz, nx, ns * own, width))
    del leaving
    qkv_sum = lax.psum_scatter(
        after(qkv_mine, in_sum, da_got), "z", scatter_dimension=0, tiled=True
    )
    qkv_z = qkv_sum
    da = da + da_got.astype(F32)
    back = jnp.concatenate([down_sum.reshape(1, ng, own, ff), in_sum.reshape(2, ng, own, ff)])
    back = exchange(back.transpose(1, 0, 2, 3), group)
    order = np.argsort(order_of(sizes)).tolist()
    qkv_sum = exchange(after(qkv_sum, wo_mine).reshape(ns, own, width), ("y", "c"))
    grad_wg, grad_wu, grad_wd = [unpack(back, m, order) for m in (1, 2, 0)]
    own_term = after(blocks[0], grad_qkv).astype(F32) + others[0].astype(F32)
    if both:
        ffn = own_term + jnp.concatenate(
            [
                up_got.astype(F32) + x_got.astype(F32),
                low_got.astype(F32) + y_got.astype(F32),
            ],
            axis=0,
        )
    else:
        ffn = ring_sum([own_term] + first, "y")
    output = (residual + ffn).astype(BF)
    x_own = tokens.astype(F32)
    inv_own = inverse_rms(x_own)
    grad_tokens = dr + rms_back(da * gain_one, x_own * inv_own, inv_own)
    wo_sum = lax.psum_scatter(
        after(wo_mine, qkv_z, grad_tokens, output), "z", scatter_dimension=0, tiled=True
    )

    qkv_sum = qkv_sum.reshape(ny, nc, own, width).transpose(2, 1, 0, 3)
    qkv_sum = qkv_sum.reshape(own, ns, width).astype(F32)
    grad_wq = qkv_sum[:, :, : heads * fk].reshape(wq.shape)
    grad_wk = qkv_sum[:, :, heads * fk : 2 * heads * fk].reshape(wk.shape)
    grad_wv = qkv_sum[:, :, 2 * heads * fk :].reshape(wv.shape)
    if joint_form:
        grad_wo = wo_sum.astype(F32)
    else:
        grad_wo = lax.ppermute(wo_sum, everything, [(t, s) for s, t in perm]).astype(F32)

    def gain_grad(gain, *pairs):
        total = sum(jnp.sum(w.astype(BF).astype(F32) * g, axis=1) for w, g in pairs)
        return total / gain.astype(BF).astype(F32)

    return (
        output,
        grad_tokens,
        grad_wq,
        grad_wk,
        grad_wv,
        grad_wo,
        grad_wg,
        grad_wu,
        grad_wd,
        gain_grad(g1, (wq, grad_wq), (wk, grad_wk), (wv, grad_wv)),
        gain_grad(g2, (wg, grad_wg), (wu, grad_wu)),
    )


def solution(mesh):
    n_dp, n_seq = mesh.shape["dp"], mesh.shape["seq"]
    nz = 4 if n_dp % 4 == 0 else n_dp
    nc = 2 if n_seq % 2 == 0 else 1
    nx, ny = n_dp // nz, n_seq // nc
    fine = Mesh(mesh.devices.reshape(nz, nx, ny, nc), ("z", "x", "y", "c"))
    both = nx == 2 and ny == 2
    all_rows = P(("z", "x", "y", "c"), None)
    vector = P(("z", "x", "y", "c"))
    placed = (
        (all_rows, P(("z", "x"), ("y", "c")), all_rows) + (all_rows,) * 7 + (vector, vector)
    )

    def run(*args):
        return per_device(both, *args)

    return jax.shard_map(
        run,
        mesh=fine,
        in_specs=placed,
        out_specs=(all_rows,) * 9 + (vector, vector),
        check_vma=False,
    )
```

```python
import functools

import jax
import jax.numpy as jnp
import numpy as np
from jax import lax
from jax.experimental import pallas as pl
from jax.experimental.pallas import tpu as pltpu
from jax.sharding import Mesh
from jax.sharding import PartitionSpec as P

HEADS = 16
EPSILON = 1e-06
BF = jnp.bfloat16
F32 = jnp.float32


def index(ax):
    return lax.axis_index(ax)


def shift(v, ax, k=1):
    n = lax.axis_size(ax)
    return lax.ppermute(v, ax, [(i, (i + k) % n) for i in range(n)])


def absolute(rel, ax):
    n = len(rel)
    if n == 1:
        return list(rel)
    i = index(ax)
    out = []
    for j in range(n):
        picked = rel[0]
        for k in range(1, n):
            picked = jnp.where((i - j + n) % n == k, rel[k], picked)
        out.append(picked)
    return out


def ring(v, ax):
    out = [v]
    for _ in range(lax.axis_size(ax) - 1):
        out.append(shift(out[-1], ax))
    return out


def ring_sum(pieces, ax):
    acc = None
    for k in range(len(pieces) - 1, 0, -1):
        term = pieces[k].astype(F32)
        if acc is not None:
            term = term + acc
        acc = shift(term.astype(BF), ax, -1).astype(F32)
    own = pieces[0].astype(F32)
    return own if acc is None else own + acc


def fan(v, ax):
    return [v] + [shift(v, ax, k) for k in range(1, lax.axis_size(ax))]


def exchange(blocks, axes):
    return lax.all_to_all(blocks, axes, 0, 0, tiled=True)


def cost(flops, nbytes):
    return pl.CostEstimate(flops=int(flops), bytes_accessed=int(nbytes), transcendentals=0)


def nothing(*refs):
    del refs


def after(v, *deps):
    return pl.pallas_call(
        nothing,
        out_shape=jax.ShapeDtypeStruct(v.shape, v.dtype),
        in_specs=[pl.BlockSpec(memory_space=pl.ANY)] * (1 + len(deps)),
        out_specs=pl.BlockSpec(memory_space=pl.ANY),
        input_output_aliases={0: 0},
        compiler_params=params(1),
        cost_estimate=cost(1, 1),
        name="after",
    )(v, *deps)


def stream_gather(v, ax_y="y", ax_c="c"):
    return [ring(piece, ax_c) for piece in ring(v, ax_y)]


def place_of(ry, rc):
    ny, nc = lax.axis_size("y"), lax.axis_size("c")
    return ((index("y") - ry + ny) % ny) * nc + (index("c") - rc + nc) % nc


def in_order(pieces):
    ny, nc = len(pieces), len(pieces[0])
    rows = pieces[0][0].shape[0]
    out = jnp.zeros((ny * nc * rows,) + pieces[0][0].shape[1:], pieces[0][0].dtype)
    for ry in range(ny):
        for rc in range(nc):
            out = lax.dynamic_update_slice_in_dim(out, pieces[ry][rc], place_of(ry, rc) * rows, 0)
    return out


def stream_sum(partial, rows):
    nc, ny = lax.axis_size("c"), lax.axis_size("y")
    sums = []
    for ry in range(ny):
        terms = [
            lax.dynamic_slice_in_dim(partial, place_of(ry, rc) * rows, rows, 0) for rc in range(nc)
        ]
        sums.append(ring_sum(terms, "c"))
    if ny == 1:
        return sums[0], jnp.zeros_like(sums[0], BF)
    acc = sums[-1]
    for k in range(ny - 2, 0, -1):
        acc = sums[k] + shift(acc.astype(BF), "y", -1).astype(F32)
    return sums[0], shift(acc.astype(BF), "y", -1)


def wide_gather(v, both):
    if both:
        half = v.shape[0] // 2
        x, y = shift(v, "x"), shift(v, "y")
        groups = [[v], [x], [y], [shift(x[:half], "y"), shift(y[half:], "x")]]
    else:
        groups = [[piece] for piece in ring(v, "y")]
    return groups


def with_other(g):
    return (g, [shift(p, "c") for p in g])


def dot(a, b, dims, out=F32):
    return lax.dot_general(a, b, (dims, ((), ())), preferred_element_type=F32).astype(out)


NN = ((1,), (0,))
NT = ((1,), (1,))
TN = ((0,), (0,))


def inverse_rms(v):
    return lax.rsqrt(jnp.mean(v * v, axis=-1, keepdims=True) + EPSILON)


def rms_back(grad, normed, inverse):
    return inverse * (grad - normed * jnp.mean(grad * normed, axis=-1, keepdims=True))


def params(limit=60):
    return pltpu.CompilerParams(vmem_limit_bytes=limit << 20)


def block_of(stream):
    return 256 if stream % 256 == 0 else stream


def allowed_of(doc_col, doc_row, r0, block, length):
    rows = r0 + lax.broadcasted_iota(jnp.int32, (block, length), 0)
    cols = lax.broadcasted_iota(jnp.int32, (block, length), 1)
    return (doc_col == doc_row) & (cols <= rows)


def head_lanes(a, h, fk):
    lane = lax.broadcasted_iota(jnp.int32, a.shape, 1)
    return jnp.where((lane >= h * fk) & (lane < (h + 1) * fk), a, jnp.zeros_like(a))


def attention_kernel(heads, fk, fv, qkv, doc_row, doc_col, att, out, den):
    stream = qkv.shape[0]
    block = block_of(stream)
    wide = heads * fk
    for r0 in range(0, stream, block):
        length = r0 + block
        rows = slice(r0, length)
        allowed = allowed_of(doc_col[rows, :], doc_row[:, :length], r0, block, length)
        q = qkv[rows, :wide]
        k = qkv[:length, wide : 2 * wide]
        dens = []
        for h in range(heads):
            at = slice(h * fv, (h + 1) * fv)
            v = qkv[:length, 2 * wide + h * fv : 2 * wide + (h + 1) * fv]
            w = 1.0 + 0.25 * dot(head_lanes(q, h, fk), k, NT)
            scores = jnp.where(allowed, 0.5 * w * w + 0.5, 0.0)
            total = jnp.sum(scores, axis=1, keepdims=True)
            o = dot(scores.astype(BF), v, NN) / total
            out[rows, at] = o
            att[rows, at] = o.astype(BF)
            dens.append(total)
        den[rows, :] = jnp.concatenate(dens, axis=1)


def attention(qkv, doc, heads, fk, fv):
    stream = qkv.shape[0]
    return pl.pallas_call(
        functools.partial(attention_kernel, heads, fk, fv),
        out_shape=(
            jax.ShapeDtypeStruct((stream, heads * fv), BF),
            jax.ShapeDtypeStruct((stream, heads * fv), F32),
            jax.ShapeDtypeStruct((stream, heads), F32),
        ),
        compiler_params=params(),
        cost_estimate=cost(2 * heads * stream * stream * 256, stream * 6000),
        name="attention",
    )(qkv, doc[None, :], doc[:, None])


def attention_back_kernel(heads, fk, fv, qkv, doc_row, doc_col, out, den, grad, dqkv, dk, dv):
    stream = qkv.shape[0]
    block = block_of(stream)
    wide = heads * fk
    for r0 in range(stream - block, -1, -block):
        length = r0 + block
        rows = slice(r0, length)
        first = length == stream
        allowed = allowed_of(doc_col[rows, :], doc_row[:, :length], r0, block, length)
        q = qkv[rows, :wide]
        k = qkv[:length, wide : 2 * wide]
        dq = jnp.zeros((block, wide), F32)
        dk_add = jnp.zeros((length, wide), F32)
        for h in range(heads):
            at = slice(h * fv, (h + 1) * fv)
            v = qkv[:length, 2 * wide + h * fv : 2 * wide + (h + 1) * fv]
            q_head = head_lanes(q, h, fk)
            w = 1.0 + 0.25 * dot(q_head, k, NT)
            scores = jnp.where(allowed, 0.5 * w * w + 0.5, 0.0).astype(BF)
            inv = 1.0 / den[rows, h : h + 1]
            g = grad[rows, at].astype(F32)
            dnum = (g * inv).astype(BF)
            dden = -jnp.sum(g * out[rows, at], axis=1, keepdims=True) * inv
            ds = dot(dnum, v, NT) + dden
            du = jnp.where(allowed, ds * (0.25 * w), 0.0).astype(BF)
            dq = dq + dot(du, head_lanes(k, h, fk), NN)
            dk_add = dk_add + dot(du, q_head, TN)
            dv_add = dot(scores, dnum, TN)
            dv[:length, at] = dv_add if first else dv[:length, at] + dv_add
        dk[:length, :] = dk_add if first else dk[:length, :] + dk_add
        dqkv[rows, :wide] = dq.astype(BF)
    dqkv[:, wide : 2 * wide] = dk[...].astype(BF)
    dqkv[:, 2 * wide :] = dv[...].astype(BF)


def attention_back(qkv, doc, out, den, grad, heads, fk, fv):
    stream = qkv.shape[0]
    return pl.pallas_call(
        functools.partial(attention_back_kernel, heads, fk, fv),
        out_shape=jax.ShapeDtypeStruct(qkv.shape, BF),
        scratch_shapes=[
            pltpu.VMEM((stream, heads * fk), F32),
            pltpu.VMEM((stream, heads * fv), F32),
        ],
        compiler_params=params(),
        cost_estimate=cost(2 * heads * stream * stream * 640, stream * 8000),
        name="attention_back",
    )(qkv, doc[None, :], doc[:, None], out, den, grad)


def qkv_in_kernel(places, at, *refs):
    n = places.shape[0]
    pieces, parts = refs[:n], refs[n : n + 2]
    a_out, qkv_out, w, gains, a_ref = refs[-5:]
    nz, _, main = parts[0].shape
    own = parts[0].shape[1] - 80
    quarter = own // 4

    @pl.when(pl.program_id(0) == 0)
    def _():
        for z in range(nz):
            for k, part in enumerate(parts):
                base = pl.multiple_of((2 * z + at[k]) * own, own)
                w[pl.ds(base, own), :main] = part[z, :own, :]
                rows = part[z, own + 64 : own + 80, :].astype(F32)
                g = []
                for t in range(4):
                    there = pl.multiple_of(base + quarter * t, quarter)
                    lanes = slice(128 * t, 128 * (t + 1))
                    w[pl.ds(there, quarter), main:] = part[z, own : own + quarter, lanes]
                    g.append((rows[:1, 128 * t :][:, :64], rows[:1, 128 * t + 64 :][:, :64]))
                for m in range(2):
                    gains[m : m + 1, pl.ds(base, own)] = jnp.concatenate([p[m] for p in g], axis=1)

    for k, piece in enumerate(pieces):

        @pl.when(pl.program_id(0) == k)
        def _(piece=piece):
            x = piece[...].astype(F32)
            a_ref[...] = (x * inverse_rms(x) * gains[:1, :]).astype(BF)

    a = a_ref[...]
    a_out[...] = a
    qkv_out[...] = dot(a, w[...], NN, BF)


def qkv_in(pieces, places, parts, at):
    n = len(pieces)
    rows, d = pieces[0].shape
    width = parts[0].shape[2] + 128

    def row_block(i, places, at):
        return (places[i], 0)

    def still(a):
        zeros = (0,) * len(a.shape)
        return pl.BlockSpec(a.shape, lambda i, places, at: zeros, pipeline_mode=pl.Buffered(1))

    def fixed(i, places, at):
        return (0, 0)

    return pl.pallas_call(
        qkv_in_kernel,
        grid_spec=pltpu.PrefetchScalarGridSpec(
            num_scalar_prefetch=2,
            grid=(n,),
            in_specs=[still(p) for p in pieces] + [still(p) for p in parts],
            out_specs=(
                pl.BlockSpec((rows, d), row_block),
                pl.BlockSpec((rows, width), row_block),
                pl.BlockSpec((d, width), fixed),
                pl.BlockSpec((2, d), fixed),
            ),
            scratch_shapes=[pltpu.VMEM((rows, d), BF)],
        ),
        out_shape=(
            jax.ShapeDtypeStruct((n * rows, d), BF),
            jax.ShapeDtypeStruct((n * rows, width), BF),
            jax.ShapeDtypeStruct((d, width), BF),
            jax.ShapeDtypeStruct((2, d), F32),
        ),
        compiler_params=params(),
        cost_estimate=cost(2 * n * rows * d * width, 6 * n * rows * d),
        name="qkv_in",
    )(places, at, *pieces, *parts)


def norm_in_kernel(places, *refs):
    pieces, gain = refs[: places.shape[0]], refs[places.shape[0]]
    a_out = refs[-1]
    for k, piece in enumerate(pieces):

        @pl.when(pl.program_id(0) == k)
        def _(piece=piece):
            x = piece[...].astype(F32)
            a_out[...] = (x * inverse_rms(x) * gain[...]).astype(BF)


def norm_in(pieces, places, gain):
    n = len(pieces)
    rows, d = pieces[0].shape

    def at(i, places):
        return (places[i], 0)

    def still(a):
        return pl.BlockSpec(a.shape, lambda i, places: (0, 0), pipeline_mode=pl.Buffered(1))

    return pl.pallas_call(
        norm_in_kernel,
        grid_spec=pltpu.PrefetchScalarGridSpec(
            num_scalar_prefetch=1,
            grid=(n,),
            in_specs=[still(p) for p in pieces] + [still(gain)],
            out_specs=pl.BlockSpec((rows, d), at),
        ),
        out_shape=jax.ShapeDtypeStruct((n * rows, d), BF),
        compiler_params=params(),
        cost_estimate=cost(n * rows * d, 4 * n * rows * d),
        name="norm_in",
    )(places, *pieces, gain)


def whole(a):
    rank = len(a.shape)
    return pl.BlockSpec(a.shape, lambda i: (0,) * rank, pipeline_mode=pl.Buffered(1))


def mat(m, w):
    parts, _, rows, cols = w.shape
    return pl.BlockSpec(
        (parts, 1, rows, cols), lambda i: (0, m, 0, 0), pipeline_mode=pl.Buffered(1)
    )


def rows_of(ref):
    parts, _, rows, cols = ref.shape
    return ref[...].reshape(parts * rows, cols)


def size_of(w):
    parts, _, rows, cols = w.shape
    return parts * rows, cols


def ffn_in_kernel(counts, *refs):
    n = sum(counts)
    parts, (wg, wu) = refs[:n], refs[n : n + 2]
    b_out, gate_out, up_out, h_out, b_ref = refs[-5:]
    start = 0
    for step, count in enumerate(counts):

        @pl.when(pl.program_id(0) == step)
        def _(some=parts[start : start + count]):
            at = 0
            for p in some:
                b_ref[at : at + p.shape[0], :] = p[...]
                at += p.shape[0]

        start += count
    b = b_ref[...]
    b_out[...] = b
    gate = dot(b, rows_of(wg), NN)
    up = dot(b, rows_of(wu), NN)
    gate_out[...] = gate
    up_out[...] = up
    h_out[...] = (gate * jax.nn.sigmoid(gate) * up).astype(BF)


def ffn_in(first, total, steps, w, buffers):
    block = sum(p.shape[0] for p in steps[0])
    d, ff = size_of(w)
    parts = [p for some in steps for p in some]
    operands = parts + [w, w]
    in_specs = [whole(p) for p in parts] + [mat(0, w), mat(1, w)]
    aliases = {}
    if buffers is not None:
        aliases = {len(operands) + j: j for j in range(4)}
        operands += list(buffers)
        in_specs += [pl.BlockSpec(memory_space=pl.ANY)] * 4
    widths = ((d, BF), (ff, F32), (ff, F32), (ff, BF))
    return pl.pallas_call(
        functools.partial(ffn_in_kernel, [len(some) for some in steps]),
        grid=(len(steps),),
        in_specs=in_specs,
        out_specs=tuple(pl.BlockSpec((block, w), lambda i: (first + i, 0)) for w, _ in widths),
        out_shape=tuple(jax.ShapeDtypeStruct((total, w), t) for w, t in widths),
        scratch_shapes=[pltpu.VMEM((block, d), BF)],
        input_output_aliases=aliases,
        compiler_params=params(),
        cost_estimate=cost(
            4 * len(steps) * block * d * ff, 4 * d * ff + len(steps) * block * (4 * d + 10 * ff)
        ),
        name="ffn_in",
    )(*operands)


def ffn_mid_kernel(gate, up, dy, wd, dg_out, du_out):
    sig = jax.nn.sigmoid(gate[...])
    dh = dot(dy[...], rows_of(wd), NN)
    dg_out[...] = (dh * up[...] * (sig * (1.0 + gate[...] * (1.0 - sig)))).astype(BF)
    du_out[...] = (dh * gate[...] * sig).astype(BF)


def ffn_mid(block, gate, up, dy, w):
    total, ff = gate.shape
    d = dy.shape[1]

    def at(i):
        return (i, 0)

    return pl.pallas_call(
        ffn_mid_kernel,
        grid=(total // block,),
        in_specs=[pl.BlockSpec((block, n), at) for n in (ff, ff, d)] + [mat(2, w)],
        out_specs=(pl.BlockSpec((block, ff), at),) * 2,
        out_shape=(jax.ShapeDtypeStruct((total, ff), BF),) * 2,
        compiler_params=params(),
        cost_estimate=cost(2 * total * d * ff, 2 * d * ff + total * (2 * d + 12 * ff)),
        name="ffn_mid",
    )(gate, up, dy, w)


def ffn_back_kernel(dgate, dup, wg, wu, *outs):
    db = dot(dgate[...], rows_of(wg), NT) + dot(dup[...], rows_of(wu), NT)
    db = db.astype(BF)
    for step, out in enumerate(outs):

        @pl.when(pl.program_id(0) == step)
        def _(out=out):
            out[...] = db


def ffn_back(first, count, block, dgate, dup, w):
    d, ff = size_of(w)
    rows = pl.BlockSpec((block, ff), lambda i: (first + i, 0))
    return pl.pallas_call(
        ffn_back_kernel,
        grid=(count,),
        in_specs=[rows, rows, mat(0, w), mat(1, w)],
        out_specs=(pl.BlockSpec((block, d), lambda i: (0, 0)),) * count,
        out_shape=(jax.ShapeDtypeStruct((block, d), BF),) * count,
        compiler_params=params(),
        cost_estimate=cost(4 * count * block * d * ff, 4 * d * ff + count * block * (2 * d + 4 * ff)),
        name="ffn_back",
    )(dgate, dup, w, w)


def dz_in_kernel(places, *refs):
    pieces, mat = refs[: places.shape[0]], refs[places.shape[0]]
    dz_out, dc_out = refs[-2:]
    for k, piece in enumerate(pieces):

        @pl.when(pl.program_id(0) == k)
        def _(piece=piece):
            dz_out[...] = piece[...]
            cols = mat.shape[3]
            dc_out[...] = sum(
                dot(piece[:, k * cols : (k + 1) * cols], columns_of(mat, k), NT)
                for k in range(mat.shape[1])
            )


def dz_in(pieces, places, mat):
    n = len(pieces)
    rows, d = pieces[0].shape
    width = mat.shape[0] * mat.shape[2]

    def at(i, places):
        return (places[i], 0)

    def still(a):
        zeros = (0,) * len(a.shape)
        return pl.BlockSpec(a.shape, lambda i, places: zeros, pipeline_mode=pl.Buffered(1))

    return pl.pallas_call(
        dz_in_kernel,
        grid_spec=pltpu.PrefetchScalarGridSpec(
            num_scalar_prefetch=1,
            grid=(n,),
            in_specs=[still(p) for p in pieces] + [still(mat)],
            out_specs=(pl.BlockSpec((rows, d), at), pl.BlockSpec((rows, width), at)),
        ),
        out_shape=(
            jax.ShapeDtypeStruct((n * rows, d), BF),
            jax.ShapeDtypeStruct((n * rows, width), F32),
        ),
        compiler_params=params(),
        cost_estimate=cost(2 * n * rows * d * width, 6 * n * rows * d),
        name="dz_in",
    )(places, *pieces, mat)


def weight_grad_kernel(a, b, out):
    out[...] = dot(a[...], b[...], TN, BF)


def weight_grad(a, b):
    rows, m = a.shape
    n = b.shape[1]
    block = 512 if m % 512 == 0 else m
    return pl.pallas_call(
        weight_grad_kernel,
        grid=(m // block,),
        in_specs=[pl.BlockSpec((rows, block), lambda i: (0, i)), whole(b)],
        out_specs=pl.BlockSpec((block, n), lambda i: (i, 0)),
        out_shape=jax.ShapeDtypeStruct((m, n), BF),
        compiler_params=params(),
        cost_estimate=cost(2 * rows * m * n, 2 * (rows * (m + n) + m * n)),
        name="weight_grad",
    )(a, b)


def pack_kernel(order, n_plain, *refs):
    out, plain, extra = refs[-1], refs[:n_plain], refs[n_plain:-1]
    rows = plain[0].shape[0]
    n = len(order)
    width = out.shape[2]
    for t, u in enumerate(order):
        some = []
        for ref in plain:
            cols = ref.shape[1] // n
            some.append(ref[:, u * cols : (u + 1) * cols].astype(BF))
        out[t, :rows, :] = jnp.concatenate(some, axis=1)
        some = []
        for ref in extra:
            gap = jnp.zeros((1, width - ref.shape[1]), F32)
            row = jnp.concatenate([ref[...], gap], axis=1) if gap.shape[1] else ref[...]
            some.append(jnp.broadcast_to(row, (8, width)))
        out[t, rows:, :] = jnp.concatenate(some, axis=0).astype(BF)


def pack_columns(order, plain, extra):
    rows = plain[0].shape[0]
    width = sum(w.shape[1] for w in plain) // len(order)
    tall = rows + 8 * len(extra)
    return pl.pallas_call(
        functools.partial(pack_kernel, order, len(plain)),
        out_shape=jax.ShapeDtypeStruct((len(order), tall, width), BF),
        compiler_params=params(),
        cost_estimate=cost(1, 6 * len(order) * tall * width),
        name="pack",
    )(*plain, *extra)


def split_kernel(order, *refs):
    out = refs[-1]
    for m, ref in enumerate(refs[:-1]):
        cols = ref.shape[1] // len(order)
        for t, u in enumerate(order):
            out[t, m] = ref[:, u * cols : (u + 1) * cols].astype(BF)


def split_columns(order, mats):
    rows, cols = mats[0].shape
    n = len(order)
    return pl.pallas_call(
        functools.partial(split_kernel, order),
        out_shape=jax.ShapeDtypeStruct((n, len(mats), rows, cols // n), BF),
        compiler_params=params(),
        cost_estimate=cost(1, 6 * len(mats) * rows * cols),
        name="split",
    )(*mats)


def down_kernel(dy, hid, hid_rows, wd, grad, *terms):
    grad[...] = dot(dy[...], hid[...], TN, BF)
    term = dot(hid_rows[...], rows_of(wd), NT, BF)
    for step, out in enumerate(terms):

        @pl.when(pl.program_id(0) == step)
        def _(out=out):
            out[...] = term


def down_both(dy, hid, w):
    rows, d = dy.shape
    ff = hid.shape[1]
    steps = 8
    return pl.pallas_call(
        down_kernel,
        grid=(steps,),
        in_specs=[
            pl.BlockSpec((rows, d // steps), lambda i: (0, i)),
            whole(hid),
            pl.BlockSpec((rows // steps, ff), lambda i: (i, 0)),
            mat(2, w),
        ],
        out_specs=(
            pl.BlockSpec((d // steps, ff), lambda i: (i, 0)),
        )
        + (pl.BlockSpec((rows // steps, d), lambda i: (0, 0)),) * steps,
        out_shape=(jax.ShapeDtypeStruct((d, ff), BF),)
        + (jax.ShapeDtypeStruct((rows // steps, d), BF),) * steps,
        compiler_params=params(),
        cost_estimate=cost(4 * rows * d * ff, 4 * (rows * d + rows * ff + d * ff)),
        name="down_both",
    )(dy, hid, hid, w)


def pair_grad_kernel(a, b0, b1, out, mark):
    mark[...] = jnp.zeros_like(mark)
    out[0, 0] = dot(a[...], b0[...], TN, BF)
    out[0, 1] = dot(a[...], b1[...], TN, BF)


def pair_grad(a, b0, b1, parts):
    rows, m = a.shape
    n = b0.shape[1]
    block = m // parts
    return pl.pallas_call(
        pair_grad_kernel,
        grid=(parts,),
        in_specs=[pl.BlockSpec((rows, block), lambda i: (0, i)), whole(b0), whole(b1)],
        out_specs=(
            pl.BlockSpec((1, 2, block, n), lambda i: (i, 0, 0, 0)),
            pl.BlockSpec((8, 128), lambda i: (0, 0)),
        ),
        out_shape=(
            jax.ShapeDtypeStruct((parts, 2, block, n), BF),
            jax.ShapeDtypeStruct((8, 128), F32),
        ),
        compiler_params=params(),
        cost_estimate=cost(4 * rows * m * n, 2 * (rows * (m + 2 * n) + 2 * m * n)),
        name="pair_grad",
    )(a, b0, b1)


def columns_of(w, k):
    n, _, rows, cols = w.shape
    return w[:, k].reshape(n * rows, cols)


def out_kernel(a, w, out):
    out[...] = jnp.concatenate(
        [dot(a[...], columns_of(w, k), NN, BF) for k in range(w.shape[1])], axis=1
    )


def out_terms(a, w):
    stream, n = a.shape
    d = w.shape[1] * w.shape[3]
    block = stream // 4
    return pl.pallas_call(
        out_kernel,
        grid=(4,),
        in_specs=[pl.BlockSpec((block, n), lambda i: (i, 0)), whole(w)],
        out_specs=pl.BlockSpec((block, d), lambda i: (i, 0)),
        out_shape=jax.ShapeDtypeStruct((stream, d), BF),
        compiler_params=params(),
        cost_estimate=cost(2 * stream * n * d, 2 * (stream * (n + d) + n * d)),
        name="out_terms",
    )(a, w)


def unpack_kernel(order, g, out):
    out[...] = jnp.concatenate([g[t, 0].astype(F32) for t in order], axis=1)


def unpack(g, m, order):
    n, _, rows, cols = g.shape
    return pl.pallas_call(
        functools.partial(unpack_kernel, order),
        grid=(1,),
        in_specs=[pl.BlockSpec((n, 1, rows, cols), lambda i: (0, m, 0, 0))],
        out_specs=pl.BlockSpec((rows, n * cols), lambda i: (0, 0)),
        out_shape=jax.ShapeDtypeStruct((rows, n * cols), F32),
        compiler_params=params(),
        cost_estimate=cost(1, 6 * n * rows * cols),
        name="unpack",
    )(g)


def sum_rows(g):
    nx = lax.axis_size("x")
    x = index("x")
    terms = [lax.dynamic_index_in_dim(g, (x - k + nx) % nx, 1, False) for k in range(nx)]
    mine = ring_sum(terms, "x").astype(BF)
    return terms[-1], mine.reshape(-1, mine.shape[-1])


def per_device(both, tokens, segments, cotangent, wq, wk, wv, wo, wg, wu, wd, g1, g2):
    rows, d = tokens.shape
    everything = ("z", "x", "y", "c")
    nz, nx, ny, nc = (lax.axis_size(a) for a in everything)
    ns = ny * nc
    stream = rows * ns
    heads = HEADS // ns
    fk = wq.shape[1] // HEADS
    fv = wv.shape[1] // HEADS
    own = wq.shape[0]

    def order_of(sizes):
        order = np.arange(int(np.prod(sizes))).reshape(sizes[::-1])
        return order.transpose().reshape(-1).tolist()

    width = (wq.shape[1] + wk.shape[1] + wv.shape[1]) // ns
    pack = pack_columns(
        order_of((ny, nc)),
        (wq, wk, wv),
        (jnp.concatenate([g1, g2])[None], segments.astype(F32)),
    )
    pack = exchange(pack, ("y", "c"))
    doc = pack[:, own + 8, :rows].astype(jnp.int32).reshape(stream)

    group = ("x", "y", "c") if both else ("y", "c")
    sizes = (nx, ny, nc) if both else (ny, nc)
    ng = nx * ns if both else ns
    ff = wg.shape[1] // ng
    along = ("z",) if both else ("z", "x")
    na = nz if both else nz * nx
    blocks = split_columns(order_of(sizes), (wg, wu, wd))
    dy_x = shift(cotangent, "x")
    vy = ring(after(tokens, pack, dy_x), "y")
    exchanged = exchange(blocks, group)
    got = exchanged.transpose(1, 0, 2, 3).reshape(-1, ff)

    ndp = nz * nx

    def gather(w, axes):
        return lax.all_gather(w, axes, axis=0, tiled=True)

    def by_x(pieces):
        return jnp.concatenate(absolute([p[:, None] for p in pieces], "x"), axis=1)

    joint_form = ns == nz == 4 and nx == 2 and own == 64 and width == 640 and d % 512 == 0
    if joint_form:
        left = jnp.concatenate([pack[t, :own, 512:] for t in range(ns)], axis=1)
        extra = jnp.concatenate([pack[t, own : own + 8, :128] for t in range(ns)], axis=1)
        some = [wo[:, k : k + 512].astype(BF) for k in range(0, d, 512)]
        stacked = [pack[:, :own, :512].reshape(ns * own, 512), left, extra, extra] + some
        joint = gather(jnp.concatenate(stacked, axis=0), "z").reshape(nz, -1, 512)
        cut = ns * own + own + 16
        qkv_parts = ring(joint[:, :cut], "x")
        units = [order_of((ny, nc))[t % ns] for t in range(nx * ns)]
        out_w = jnp.stack([joint[u, cut:] for u in units])
        out_w = exchange(after(out_w, qkv_parts[-1]), ("x", "y", "c"))
        out_w = out_w.reshape(nx * ns, d // 512, own, 512)
        arrived_last = [joint]

    else:
        perm = []
        for dp in range(ndp):
            for u in range(ns):
                perm.append((u * ndp + dp, dp * ns + u % ny * nc + u // ny))
        tall = ns * (own + 8)
        qkv_z = gather(pack[:, : own + 8].reshape(tall, width), "z")
        out_z = gather(lax.ppermute(wo.astype(BF), everything, perm), "z")
        qkv_parts = ring(qkv_z.reshape(nz, tall, width), "x")
        out_w = by_x(ring(out_z.reshape(nz, own, d), "x"))
        out_w = out_w.reshape(1, -1, d // 256, 256).transpose(0, 2, 1, 3)
        arrived_last = [qkv_z, out_z]

    got = after(got, vy[-1], dy_x, *arrived_last)
    ffn_w = gather(got, along).reshape(na, 3, d // na, ff)
    x_pieces = [ring(p, "c") for p in vy]
    places = jnp.stack([place_of(ry, rc) for ry in range(ny) for rc in range(nc)])
    flat = [p for some in x_pieces for p in some]
    if joint_form:
        at = jnp.stack([index("x"), 1 - index("x")])
        a_all, qkv, qkv_mat, gains = qkv_in(flat, places, qkv_parts, at)
        gain_one, gain_two = gains[:1], gains[1:]
    else:
        qkv_all = by_x(qkv_parts).reshape(ndp * ns, own + 8, width)
        qkv_mat = qkv_all[:, :own].reshape(d, width)
        gains = qkv_all[:, own, : 2 * own].astype(F32)
        gain_one, gain_two = gains[:, :own].reshape(1, d), gains[:, own:].reshape(1, d)
        a_all = norm_in(flat, places, gain_one)
        qkv = dot(a_all, qkv_mat, NN, BF)
    late = after(cotangent, exchanged)
    if both:
        half = rows // 2
        dy_x, dy_y = after(dy_x, qkv_parts[-1]), after(shift(late, "y"), qkv_parts[-1])
        dy_near = [dy_y]
        dy_far = [shift(dy_x[:half], "y"), shift(dy_y[half:], "x")]
        dy_groups = [[late], [dy_x], [dy_y], dy_far]
    else:
        dy_groups = [[p] for p in ring(late, "y")]
        dy_near, dy_far = dy_groups[1], dy_groups[-1]
    dy_groups = [(g, [shift(p, "c") for p in g]) for g in dy_groups]
    dy_all = jnp.concatenate([p for mine, theirs in dy_groups for p in mine + theirs], axis=0)
    att, o, den = attention(qkv, doc, heads, fk, fv)
    mine, got_r = stream_sum(out_terms(after(att, *dy_near, *dy_far), out_w), rows)
    residual = tokens.astype(F32) + mine + got_r.astype(F32)
    inv_mlp = inverse_rms(residual)
    normed_res = residual * inv_mlp
    b = (normed_res * gain_two).astype(BF)

    groups = wide_gather(b, both)
    count = len(groups)
    b_far = groups[-1]
    total = 2 * count * rows
    near = [some for g in groups[:-1] for some in with_other(g)]
    near[0] = [after(near[0][0], dy_all)]
    buffers = ffn_in(0, total, near, ffn_w, None)
    b_far = with_other([after(p, buffers[3]) for p in b_far])
    buffers = ffn_in(2 * count - 2, total, list(b_far), ffn_w, buffers)
    b_all, gate, up, hidden = buffers
    dgate, dup = ffn_mid(rows, gate, up, dy_all, ffn_w)

    def back(some, dgate, *deps):
        out = ffn_back(2 * some[0], 2 * len(some), rows, dgate, dup, ffn_w)
        theirs = [after(p, *deps) if deps else p for p in out[1::2]]
        return [(m, t, shift(t, "c")) for m, t in zip(out[::2], theirs)]

    def joined(mine, _, other):
        return mine.astype(F32) + other.astype(F32)

    def send(a, ax):
        return shift(a, ax).astype(F32)

    half = rows // 2
    if both:
        far = joined(*back([3], dgate)[0]).astype(BF)
        up_got, low_got = send(far[:half], "y"), send(far[half:], "x")
        dgate = after(dgate, far)
        tx, ty = [joined(*t) for t in back([1, 2], dgate, up_got, low_got)]
        x_low, y_up = tx[half:].astype(BF), ty[:half].astype(BF)
        x_up, y_low = (tx[:half] + up_got).astype(BF), (ty[half:] + low_got).astype(BF)
        dgate = after(dgate, x_low, y_up)
        mine = back([0], dgate)[0]
        own_term = joined(*mine)
        hidden = after(hidden, x_up, y_low, own_term)
        grad_down, *blocks = down_both(dy_all, hidden, ffn_w)
        own_term = after(own_term, blocks[0])
        db = jnp.concatenate(
            [
                own_term[:half] + send(y_up, "y") + send(x_up, "x"),
                own_term[half:] + send(x_low, "x") + send(y_low, "y"),
            ],
            axis=0,
        )
    else:
        terms = [joined(*t) for t in back(list(range(count)), dgate)]
        grad_down, *blocks = down_both(dy_all, hidden, ffn_w)
        db = ring_sum(terms, "y")
    dr = cotangent.astype(F32) + rms_back(db * gain_two, normed_res, inv_mlp)

    dz = dr.astype(BF)
    down_sum = lax.psum_scatter(after(grad_down, dz), along, scatter_dimension=0, tiled=True)
    dz_y = ring(dz, "y")
    dz_own = ring(dz, "c")
    arrived = dz_y[-1]
    soon = dz_own[-1]
    others = [shift(blocks[2 * g + 1], "c") for g in range(count)]
    first = [
        (blocks[2 * g].astype(F32) + others[g].astype(F32)).astype(BF) for g in range(1, count)
    ]
    grad_in, mark = pair_grad(b_all, after(dgate, soon, *first), dup, na)
    dz_pieces = [dz_own] + [ring(after(p, mark), "c") for p in dz_y[1:]]
    dz_all, dc = dz_in([p for some in dz_pieces for p in some], places, out_w)
    far_got = shift(after(first[-1][: rows // 2], arrived), "y")
    grad_wo = weight_grad(att, after(dz_all, far_got))
    in_sum = lax.psum_scatter(
        after(grad_in.reshape(-1, ff), grad_wo, down_sum),
        along,
        scatter_dimension=0,
        tiled=True,
    )
    dc = after(dc, grad_wo)
    if both:
        to_x, to_y, far = first
        low_got = shift(to_x[half:], "x")
        y_low = (to_y[half:].astype(F32) + send(far[half:], "x")).astype(BF)
        x_up = (to_x[:half].astype(F32) + far_got.astype(F32)).astype(BF)
        up_got = shift(after(to_y[:half], arrived), "y")
        y_low = after(y_low, arrived)
        x_got, y_got = shift(x_up, "x"), shift(y_low, "y")
    ffn_got = [up_got, low_got, x_got, y_got] if both else []
    dqkv = attention_back(qkv, doc, o, den, dc, heads, fk, fv)
    dqkv = after(dqkv, *ffn_got)
    if joint_form:
        g = after(grad_wo, dqkv).reshape(nx * ns, own, d)
        wo_there = exchange(g, ("x", "y", "c"))
        g = jnp.sum(wo_there.reshape(nx, ns, own, d).astype(F32), axis=0).astype(BF)
        wo_mine = jnp.concatenate([g[t] for t in np.argsort(order_of((ny, nc)))], axis=0)
    else:
        _, wo_mine = sum_rows(grad_wo.reshape(nz, nx, own, d))
        wo_there = wo_mine
    da_part = dot(dqkv, qkv_mat, NT)
    grad_qkv = after(weight_grad(a_all, after(dqkv, da_part)), wo_there)
    da, da_got = stream_sum(da_part, rows)
    leaving, qkv_mine = sum_rows(grad_qkv.reshape(nz, nx, ns * own, width))
    del leaving
    qkv_sum = lax.psum_scatter(
        after(qkv_mine, in_sum, da_got), "z", scatter_dimension=0, tiled=True
    )
    qkv_z = qkv_sum
    da = da + da_got.astype(F32)
    back = jnp.concatenate([down_sum.reshape(1, ng, own, ff), in_sum.reshape(2, ng, own, ff)])
    back = exchange(back.transpose(1, 0, 2, 3), group)
    order = np.argsort(order_of(sizes)).tolist()
    qkv_sum = exchange(after(qkv_sum, wo_mine).reshape(ns, own, width), ("y", "c"))
    grad_wg, grad_wu, grad_wd = [unpack(back, m, order) for m in (1, 2, 0)]
    own_term = after(blocks[0], grad_qkv).astype(F32) + others[0].astype(F32)
    if both:
        ffn = own_term + jnp.concatenate(
            [
                up_got.astype(F32) + x_got.astype(F32),
                low_got.astype(F32) + y_got.astype(F32),
            ],
            axis=0,
        )
    else:
        ffn = ring_sum([own_term] + first, "y")
    output = (residual + ffn).astype(BF)
    x_own = tokens.astype(F32)
    inv_own = inverse_rms(x_own)
    grad_tokens = dr + rms_back(da * gain_one, x_own * inv_own, inv_own)
    wo_sum = lax.psum_scatter(
        after(wo_mine, qkv_z, grad_tokens, output), "z", scatter_dimension=0, tiled=True
    )

    qkv_sum = qkv_sum.reshape(ny, nc, own, width).transpose(2, 1, 0, 3)
    qkv_sum = qkv_sum.reshape(own, ns, width).astype(F32)
    grad_wq = qkv_sum[:, :, : heads * fk].reshape(wq.shape)
    grad_wk = qkv_sum[:, :, heads * fk : 2 * heads * fk].reshape(wk.shape)
    grad_wv = qkv_sum[:, :, 2 * heads * fk :].reshape(wv.shape)
    if joint_form:
        grad_wo = wo_sum.astype(F32)
    else:
        grad_wo = lax.ppermute(wo_sum, everything, [(t, s) for s, t in perm]).astype(F32)

    def gain_grad(gain, *pairs):
        total = sum(jnp.sum(w.astype(BF).astype(F32) * g, axis=1) for w, g in pairs)
        return total / gain.astype(BF).astype(F32)

    return (
        output,
        grad_tokens,
        grad_wq,
        grad_wk,
        grad_wv,
        grad_wo,
        grad_wg,
        grad_wu,
        grad_wd,
        gain_grad(g1, (wq, grad_wq), (wk, grad_wk), (wv, grad_wv)),
        gain_grad(g2, (wg, grad_wg), (wu, grad_wu)),
    )


def solution(mesh):
    n_dp, n_seq = mesh.shape["dp"], mesh.shape["seq"]
    nz = 4 if n_dp % 4 == 0 else n_dp
    nc = 2 if n_seq % 2 == 0 else 1
    nx, ny = n_dp // nz, n_seq // nc
    fine = Mesh(mesh.devices.reshape(nz, nx, ny, nc), ("z", "x", "y", "c"))
    both = nx == 2 and ny == 2
    all_rows = P(("z", "x", "y", "c"), None)
    vector = P(("z", "x", "y", "c"))
    placed = (
        (all_rows, P(("z", "x"), ("y", "c")), all_rows) + (all_rows,) * 7 + (vector, vector)
    )

    def run(*args):
        return per_device(both, *args)

    return jax.shard_map(
        run,
        mesh=fine,
        in_specs=placed,
        out_specs=(all_rows,) * 9 + (vector, vector),
        check_vma=False,
    )
```
